32 devices in a mesh: row: 4 (over y, core), col: 4 (over z), depth: 2 (over x).
Axes of the slice: x: 2, y: 2, z: 4, core: 2. Of those that a mesh axis runs over, the one named last changes fastest.
Arguments:
- tokens: bfloat16 [256, 4096], P(('col', 'depth'), 'row'), may hold values from -6 to 6
- out_grad: bfloat16 [256, 4096], P(('col', 'depth'), 'row'), may hold values from -2 to 2
- w_in: bfloat16 [4096, 14336], P('row', 'col'), may hold values from -0.09375 to 0.09375
- b_in: float32 [14336], P('col'), may hold values from -3 to 3
- w_out: bfloat16 [14336, 4096], P('col', 'row'), may hold values from -0.046875 to 0.046875
Outputs:
- block_out: bfloat16 [256, 4096], P(('col', 'depth'), 'row')
- tokens_grad: bfloat16 [256, 4096], P(('col', 'depth'), 'row')
- w_in_grad: bfloat16 [4096, 14336], P('row', ('col', 'depth'))
- w_out_grad: bfloat16 [14336, 4096], P(('col', 'depth'), 'row')
- b_in_grad: float32 [14336], P('col')
The draws below stay inside these ranges and needn't reach their ends.
All inputs are finite; a program needn't handle non-finite values.
Results may differ from the reference program's by a relative error of at most 0.005.
Values may be sent and summed in bfloat16 or wider, within the bound.
A program may use at most 64 MiB of HBM per device.

```python
import jax
import jax.numpy as jnp

D = 4096
FF = 14336
TOKENS = 256


def block_levels(rng, extent, pieces, smallest, top_value):
    def one(axis_at, shards_of):
        draws = jax.random.uniform(jax.random.fold_in(jax.random.fold_in(rng, 6), axis_at), (shards_of,), jnp.float32, smallest / len(pieces), top_value / len(pieces))
        return jnp.repeat(jnp.exp(draws), extent[axis_at] // shards_of).reshape((-1,) + (1,) * (len(extent) - axis_at - 1))

    loudness = one(*pieces[0])
    for cut in pieces[1:]:
        loudness = loudness * one(*cut)
    return loudness


def noise(own_key, extent, width, limit, split=(), held_as=jnp.bfloat16):
    loudness = block_levels(own_key, extent, split, -0.22, 0.18) if split else 1.0
    values = jax.random.normal(own_key, extent, jnp.float32) * width * loudness
    return jnp.minimum(jnp.maximum(values, -limit), limit).astype(held_as)


def setup_inputs(seed: int = 0) -> dict:
    key_of = jax.random.split(jax.random.key(seed), 6)
    return {
        "tokens": noise(key_of[0], (TOKENS, D), 1.0, 6.0, ((0, 8), (1, 4))),
        "out_grad": noise(key_of[1], (TOKENS, D), 0.3, 2.0, ((0, 8), (1, 4))),
        "w_in": noise(key_of[2], (D, FF), D ** -0.5, 0.09375, ((0, 4), (1, 4))),
        "b_in": noise(key_of[3], (FF,), 0.5, 3.0, ((0, 4),), jnp.float32),
        "w_out": noise(key_of[4], (FF, D), FF ** -0.5, 0.046875, ((0, 4), (1, 4))),
    }


root_coeff = 0.7978845608028654
cubic_coeff = 0.044715


def gelu_parts(pre_act):
    inner_arg = root_coeff * (pre_act + cubic_coeff * pre_act * pre_act * pre_act)
    tangent = jnp.tanh(inner_arg)
    gelu_value = 0.5 * pre_act * (1.0 + tangent)
    gelu_slope = 0.5 * (1.0 + tangent) + 0.5 * pre_act * (1.0 - tangent * tangent) * root_coeff * (1.0 + 3.0 * cubic_coeff * pre_act * pre_act)
    return gelu_value, gelu_slope


def reference(tokens, out_grad, w_in, b_in, w_out):
    pre_act = jnp.dot(tokens, w_in, preferred_element_type=jnp.float32) + b_in
    gelu_value, gelu_slope = gelu_parts(pre_act)
    hidden_act = gelu_value.astype(jnp.bfloat16)
    block_out = jnp.dot(hidden_act, w_out, preferred_element_type=jnp.float32).astype(jnp.bfloat16)
    act_grad = jnp.dot(out_grad, w_out.T, preferred_element_type=jnp.float32)
    pre_grad = act_grad * gelu_slope
    hidden_grad = pre_grad.astype(jnp.bfloat16)
    tokens_grad = jnp.dot(hidden_grad, w_in.T, preferred_element_type=jnp.float32).astype(jnp.bfloat16)
    w_in_grad = jnp.dot(tokens.T, hidden_grad, preferred_element_type=jnp.float32).astype(jnp.bfloat16)
    w_out_grad = jnp.dot(hidden_act.T, out_grad, preferred_element_type=jnp.float32).astype(jnp.bfloat16)
    b_in_grad = jnp.sum(pre_grad, axis=0)
    return block_out, tokens_grad, w_in_grad, w_out_grad, b_in_grad
```

```python
import functools

import jax
import jax.numpy as jnp
from jax import lax
from jax.experimental import pallas as pl
from jax.experimental.pallas import tpu as pltpu
from jax.sharding import PartitionSpec as P

root_coeff = 0.7978845608028654
cubic_coeff = 0.044715


def gelu_parts(pre_act):
    inner_arg = root_coeff * (pre_act + cubic_coeff * pre_act * pre_act * pre_act)
    tangent = jnp.tanh(inner_arg)
    gelu_value = 0.5 * pre_act * (1.0 + tangent)
    gelu_slope = 0.5 * (1.0 + tangent) + 0.5 * pre_act * (1.0 - tangent * tangent) * root_coeff * (
        1.0 + 3.0 * cubic_coeff * pre_act * pre_act
    )
    return (gelu_value, gelu_slope)


def right_transposed(left_side, right_side):
    return lax.dot_general(
        left_side, right_side, (((1,), (1,)), ((), ())), preferred_element_type=jnp.float32
    )


def left_transposed(left_side, right_side):
    return lax.dot_general(
        left_side, right_side, (((0,), (0,)), ((), ())), preferred_element_type=jnp.float32
    )


def depth_rows(gathered, col_count, depth_index, depth_count):
    tile_rows = gathered.shape[0] // (col_count * depth_count)
    shaped = gathered.reshape(col_count, depth_count, tile_rows, gathered.shape[1])
    picked = lax.dynamic_index_in_dim(shaped, depth_index, 1, keepdims=False)
    return picked.reshape(col_count * tile_rows, gathered.shape[1])


def local(tokens, out_grad, w_in, b_in, w_out):
    col_count = lax.axis_size("col")
    depth_count = lax.axis_size("depth")
    tile_rows = tokens.shape[0]
    part_cols = w_in.shape[1] // depth_count
    depth_index = lax.axis_index("depth")
    all_input, all_grad = (
        lax.all_gather(tokens, ("col", "depth"), axis=0, tiled=True),
        lax.all_gather(out_grad, ("col", "depth"), axis=0, tiled=True),
    )
    plane_input = depth_rows(all_input, col_count, depth_index, depth_count)
    plane_grad = depth_rows(all_grad, col_count, depth_index, depth_count)
    pre_sum = lax.psum_scatter(
        jnp.dot(plane_input, w_in, preferred_element_type=jnp.float32),
        "row",
        scatter_dimension=0,
        tiled=True,
    )
    pre_share = pre_sum + b_in
    gelu_value, gelu_slope = gelu_parts(pre_share)
    plane_act = lax.all_gather(gelu_value.astype(jnp.bfloat16), "row", axis=0, tiled=True)
    block_out = lax.psum_scatter(
        jnp.dot(plane_act, w_out, preferred_element_type=jnp.float32),
        "col",
        scatter_dimension=0,
        tiled=True,
    ).astype(jnp.bfloat16)
    grad_share = lax.psum_scatter(
        right_transposed(plane_grad, w_out), "row", scatter_dimension=0, tiled=True
    )
    pre_grad = grad_share * gelu_slope
    plane_hgrad = lax.all_gather(pre_grad.astype(jnp.bfloat16), "row", axis=0, tiled=True)
    b_in_grad = lax.psum(jnp.sum(pre_grad, axis=0), ("row", "depth"))
    tokens_grad = lax.psum_scatter(
        right_transposed(plane_hgrad, w_in), "col", scatter_dimension=0, tiled=True
    ).astype(jnp.bfloat16)
    act_parts = lax.all_to_all(
        plane_act.reshape(col_count, tile_rows, w_in.shape[1]),
        "depth",
        split_axis=2,
        concat_axis=1,
        tiled=True,
    )
    act_parts = act_parts.reshape(-1, part_cols)
    hgrad_parts = lax.all_to_all(
        plane_hgrad.reshape(col_count, tile_rows, w_in.shape[1]),
        "depth",
        split_axis=2,
        concat_axis=1,
        tiled=True,
    )
    hgrad_parts = hgrad_parts.reshape(-1, part_cols)
    w_in_grad = left_transposed(all_input, hgrad_parts)
    w_out_grad = left_transposed(act_parts, all_grad)
    return (
        block_out,
        tokens_grad,
        w_in_grad.astype(jnp.bfloat16),
        w_out_grad.astype(jnp.bfloat16),
        b_in_grad,
    )


MESH = pl.DeviceIdType.MESH
TILE = 256
BF16 = jnp.bfloat16
F32 = jnp.float32


def block_kernel(
    col_count,
    tokens_ref, grad_ref, w_in_ref, bias_ref, w_out_ref,
    out_ref, tgrad_ref, bgrad_ref, tok_out, og_out, act_out, hg_out,
    tok, og, w_in, w_out, part, part16, core_in, chip16, y_in, act, hg, slope,
    x_out, x_in, z_sum, z_out, z_in, b_acc, b_core, b_own, b_x,
    local_sem, z_ssem, z_rsem, x_ssem, x_rsem, c_ssem, c_rsem, y_ssem, y_rsem,
    a_ssem, a_rsem, rx_ssem, rx_rsem, rz_ssem, rz_rsem, b_ssem, b_rsem, out_sem,
):
    row = lax.axis_index("row")
    col = lax.axis_index("col")
    depth = lax.axis_index("depth")
    core = lax.rem(row, 2)
    core_peer = {"row": row + 1 - 2 * core}
    y_peer = {"row": lax.rem(row + 2, 4)}
    x_peer = {"depth": 1 - depth}
    hidden = w_in.shape[1]
    feats = w_in.shape[0]
    half = part.shape[3]

    def z_peer(step):
        return {"col": lax.rem(col + step, col_count)}

    def z_from(step):
        return lax.rem(col + col_count - step, col_count)

    def remote(src, dst, ssem, rsem, peer):
        return pltpu.make_async_remote_copy(
            src_ref=src, dst_ref=dst, send_sem=ssem, recv_sem=rsem, device_id=peer, device_id_type=MESH
        )

    base = pl.multiple_of(depth * hidden, 128)
    locals_ = [
        pltpu.make_async_copy(tokens_ref, tok.at[0, col], local_sem.at[0]),
        pltpu.make_async_copy(w_in_ref.at[:, pl.ds(base, hidden)], w_in, local_sem.at[1]),
        pltpu.make_async_copy(grad_ref, og.at[0, col], local_sem.at[2]),
        pltpu.make_async_copy(w_out_ref.at[pl.ds(base, hidden), :], w_out, local_sem.at[3]),
    ]
    for copy in locals_:
        copy.start()

    barrier = pltpu.get_barrier_semaphore()
    peers = [z_peer(step) for step in range(1, col_count)] + [x_peer, y_peer, core_peer]
    for peer in peers:
        pl.semaphore_signal(barrier, inc=1, device_id=peer, device_id_type=MESH)
    pl.semaphore_wait(barrier, len(peers))

    sends = []

    def start(copy):
        copy.start()
        sends.append(copy)
        return copy

    def gather_start(which, src, dst):
        start(remote(src, dst.at[1, col], x_ssem.at[which, 0], x_rsem.at[which, 0], x_peer))
        for step in range(1, col_count):
            start(remote(src, dst.at[0, col], z_ssem.at[which, step], z_rsem.at[which, step], z_peer(step)))

    def gather_own(which, dst):
        for step in range(1, col_count):
            block = dst.at[0, z_from(step)]
            remote(block, block, z_ssem.at[which, step], z_rsem.at[which, step], z_peer(step)).wait_recv()
            start(remote(block, dst.at[1, z_from(step)], x_ssem.at[which, step], x_rsem.at[which, step], x_peer))

    def gather_other(which, dst):
        for step in range(col_count):
            block = dst.at[1, z_from(step)]
            remote(block, block, x_ssem.at[which, step], x_rsem.at[which, step], x_peer).wait_recv()

    def tile_of(i):
        return pl.ds(pl.multiple_of(i * TILE, TILE), TILE)

    def rows_of(buf, chunk):
        value = buf[chunk]
        return value.reshape(value.shape[0] * value.shape[1], value.shape[2])

    def product(which, chunk, multiply):
        @pl.loop(0, hidden // TILE)
        def _(i):
            at = tile_of(i)
            value = multiply(at)
            for k in range(2):
                piece = value[k * half:(k + 1) * half]
                part[which, chunk, k, :, at] = piece
                part16[which, chunk, k, :, at] = piece.astype(BF16)

        start(remote(
            part16.at[which, chunk, 1 - core], core_in.at[which, chunk],
            c_ssem.at[which, chunk], c_rsem.at[which, chunk], core_peer,
        ))

    def chip_sum(which, chunk):
        landed = core_in.at[which, chunk]
        remote(landed, landed, c_ssem.at[which, chunk], c_rsem.at[which, chunk], core_peer).wait_recv()

        @pl.loop(0, hidden // TILE)
        def _(i):
            at = tile_of(i)
            total = part[which, chunk, core, :, at] + core_in[which, chunk, :, at].astype(F32)
            chip16[which, chunk, :, at] = total.astype(BF16)

        start(remote(
            chip16.at[which, chunk], y_in.at[which, chunk],
            y_ssem.at[which, chunk], y_rsem.at[which, chunk], y_peer,
        ))

    def y_wait(which, chunk):
        landed = y_in.at[which, chunk]
        remote(landed, landed, y_ssem.at[which, chunk], y_rsem.at[which, chunk], y_peer).wait_recv()

    def row_sum(which, chunk, at):
        return chip16[which, chunk, :, at].astype(F32) + y_in[which, chunk, :, at].astype(F32)

    def share_start(which, chunk, buf):
        mine = buf.at[chunk, core]
        start(remote(mine, mine, a_ssem.at[which, chunk], a_rsem.at[which, chunk], core_peer))

    def share_wait(which, chunk, buf):
        theirs = buf.at[chunk, 1 - core]
        remote(theirs, theirs, a_ssem.at[which, chunk], a_rsem.at[which, chunk], core_peer).wait_recv()

    def activate(chunk):
        y_wait(0, chunk)

        @pl.loop(0, hidden // TILE)
        def _(i):
            at = tile_of(i)
            bias = bias_ref[:, pl.ds(pl.multiple_of(depth * hidden + i * TILE, 128), TILE)]
            value, slope_here = gelu_parts(row_sum(0, chunk, at) + bias)
            act[chunk, core, :, at] = value.astype(BF16)
            slope[chunk, :, at] = slope_here

        share_start(0, chunk, act)

    def hidden_grad(chunk, first):
        y_wait(1, chunk)

        @pl.loop(0, hidden // TILE)
        def _(i):
            at = tile_of(i)
            pre_grad = row_sum(1, chunk, at) * slope[chunk, :, at]
            hg[chunk, core, :, at] = pre_grad.astype(BF16)
            total = jnp.sum(pre_grad, axis=0, keepdims=True)
            b_acc[:, at] = total if first else b_acc[:, at] + total

        share_start(1, chunk, hg)

    def project(which, chunk, buf, multiply):
        tile_rows = x_out.shape[2]

        @pl.loop(0, feats // TILE)
        def _(i):
            at = tile_of(i)
            value = multiply(rows_of(buf, chunk), at)
            for c in range(col_count):
                piece = value[c * tile_rows:(c + 1) * tile_rows]
                if chunk == 1:
                    x_out[which, c, :, at] = piece.astype(BF16)
                else:
                    z_sum[which, c, :, at] = piece

        if chunk == 1:
            start(remote(x_out.at[which], x_in.at[which], rx_ssem.at[which], rx_rsem.at[which], x_peer))

    def plane_sum(which):
        landed = x_in.at[which]
        remote(landed, landed, rx_ssem.at[which], rx_rsem.at[which], x_peer).wait_recv()
        for c in range(col_count):
            total = z_sum[which, c] + x_in[which, c].astype(F32)
            z_sum[which, c] = total
            z_out[which, c] = total.astype(BF16)
        for step in range(1, col_count):
            start(remote(
                z_out.at[which, lax.rem(col + step, col_count)], z_in.at[which, step - 1],
                rz_ssem.at[which, step - 1], rz_rsem.at[which, step - 1], z_peer(step),
            ))

    def final_sum(which, result):
        for step in range(1, col_count):
            landed = z_in.at[which, step - 1]
            remote(
                landed, landed, rz_ssem.at[which, step - 1], rz_rsem.at[which, step - 1], z_peer(step)
            ).wait_recv()
        total = z_sum[which, col]
        for step in range(1, col_count):
            total = total + z_in[which, step - 1].astype(F32)
        result[...] = total.astype(BF16)

    def keep(which, src, dst):
        copy = pltpu.make_async_copy(src, dst, out_sem.at[which])
        copy.start()
        return copy

    def pre_tile(chunk):
        return lambda at: jnp.dot(rows_of(tok, chunk), w_in[:, at], preferred_element_type=F32)

    def back_tile(chunk):
        return lambda at: right_transposed(rows_of(og, chunk), w_out[at, :])

    gather_start(0, tokens_ref, tok)
    gather_own(0, tok)
    gather_start(1, grad_ref, og)
    locals_[0].wait()
    locals_[1].wait()
    product(0, 0, pre_tile(0))
    chip_sum(0, 0)
    gather_other(0, tok)
    kept = [keep(0, tok, tok_out)]
    product(0, 1, pre_tile(1))
    chip_sum(0, 1)
    gather_own(1, og)
    locals_[2].wait()
    locals_[3].wait()
    product(1, 0, back_tile(0))
    gather_other(1, og)
    kept.append(keep(1, og, og_out))
    product(1, 1, back_tile(1))
    chip_sum(1, 1)
    chip_sum(1, 0)
    activate(0)
    activate(1)
    share_wait(0, 0, act)
    share_wait(0, 1, act)
    kept.append(keep(2, act, act_out))

    def forward(value, at):
        return jnp.dot(value, w_out[:, at], preferred_element_type=F32)

    def backward(value, at):
        return right_transposed(value, w_in[at, :])

    project(0, 1, act, forward)
    project(0, 0, act, forward)
    plane_sum(0)
    hidden_grad(1, True)
    share_wait(1, 1, hg)
    project(1, 1, hg, backward)
    hidden_grad(0, False)
    start(remote(b_acc, b_core, b_ssem.at[0], b_rsem.at[0], core_peer))
    share_wait(1, 0, hg)
    kept.append(keep(3, hg, hg_out))
    project(1, 0, hg, backward)
    plane_sum(1)
    remote(b_core, b_core, b_ssem.at[0], b_rsem.at[0], core_peer).wait_recv()
    b_own[...] = b_acc[...] + b_core[...]
    start(remote(b_own, b_x, b_ssem.at[1], b_rsem.at[1], x_peer))
    final_sum(0, out_ref)
    remote(b_x, b_x, b_ssem.at[1], b_rsem.at[1], x_peer).wait_recv()
    bgrad_ref[:, pl.ds(base, hidden)] = b_own[...]
    bgrad_ref[:, pl.ds(pl.multiple_of((1 - depth) * hidden, 128), hidden)] = b_x[...]
    final_sum(1, tgrad_ref)
    for copy in kept:
        copy.wait()
    for copy in sends:
        copy.wait_send()


def weight_kernel(tok_ref, og_ref, act_ref, hg_ref, w_in_grad_ref, w_out_grad_ref):
    w_in_grad_ref[...] = left_transposed(tok_ref[...], hg_ref[...]).astype(BF16)
    w_out_grad_ref[...] = left_transposed(act_ref[...], og_ref[...]).astype(BF16)


def fused(col_count, tokens, out_grad, w_in, b_in, w_out):
    tile_rows, feats = tokens.shape
    hidden = w_in.shape[1] // 2
    plane = col_count * tile_rows
    half = plane // 2
    rows = 2 * plane
    anywhere = pl.BlockSpec(memory_space=pl.ANY)
    vmem = pl.BlockSpec(memory_space=pltpu.VMEM)
    dma = pltpu.SemaphoreType.DMA
    outs = pl.pallas_call(
        functools.partial(block_kernel, col_count),
        out_shape=[
            jax.ShapeDtypeStruct((tile_rows, feats), BF16),
            jax.ShapeDtypeStruct((tile_rows, feats), BF16),
            jax.ShapeDtypeStruct((1, 2 * hidden), F32),
            jax.ShapeDtypeStruct((2, col_count, tile_rows, feats), BF16),
            jax.ShapeDtypeStruct((2, col_count, tile_rows, feats), BF16),
            jax.ShapeDtypeStruct((2, 2, half, hidden), BF16),
            jax.ShapeDtypeStruct((2, 2, half, hidden), BF16),
        ],
        in_specs=[anywhere, anywhere, anywhere, vmem, anywhere],
        out_specs=[vmem, vmem, vmem, anywhere, anywhere, anywhere, anywhere],
        scratch_shapes=[
            pltpu.VMEM((2, col_count, tile_rows, feats), BF16),
            pltpu.VMEM((2, col_count, tile_rows, feats), BF16),
            pltpu.VMEM((feats, hidden), BF16),
            pltpu.VMEM((hidden, feats), BF16),
            pltpu.VMEM((2, 2, 2, half, hidden), F32),
            pltpu.VMEM((2, 2, 2, half, hidden), BF16),
            pltpu.VMEM((2, 2, half, hidden), BF16),
            pltpu.VMEM((2, 2, half, hidden), BF16),
            pltpu.VMEM((2, 2, half, hidden), BF16),
            pltpu.VMEM((2, 2, half, hidden), BF16),
            pltpu.VMEM((2, 2, half, hidden), BF16),
            pltpu.VMEM((2, half, hidden), F32),
            pltpu.VMEM((2, col_count, tile_rows, feats), BF16),
            pltpu.VMEM((2, col_count, tile_rows, feats), BF16),
            pltpu.VMEM((2, col_count, tile_rows, feats), F32),
            pltpu.VMEM((2, col_count, tile_rows, feats), BF16),
            pltpu.VMEM((2, col_count - 1, tile_rows, feats), BF16),
            pltpu.VMEM((1, hidden), F32),
            pltpu.VMEM((1, hidden), F32),
            pltpu.VMEM((1, hidden), F32),
            pltpu.VMEM((1, hidden), F32),
            dma((4,)),
            dma((2, col_count)),
            dma((2, col_count)),
            dma((2, col_count)),
            dma((2, col_count)),
            dma((2, 2)),
            dma((2, 2)),
            dma((2, 2)),
            dma((2, 2)),
            dma((2, 2)),
            dma((2, 2)),
            dma((2,)),
            dma((2,)),
            dma((2, col_count - 1)),
            dma((2, col_count - 1)),
            dma((2,)),
            dma((2,)),
            dma((4,)),
        ],
        compiler_params=pltpu.CompilerParams(
            collective_id=0, has_side_effects=True, vmem_limit_bytes=44 * 2**20
        ),
        cost_estimate=pl.CostEstimate(
            flops=8 * rows * feats * hidden, bytes_accessed=8 * feats * hidden, transcendentals=rows * hidden
        ),
    )(tokens, out_grad, w_in, b_in.reshape(1, -1), w_out)
    block_out, tokens_grad, bias_grad, tok, og, act, hg = outs
    whole_block = lambda i: (0, 0)
    w_in_grad, w_out_grad = pl.pallas_call(
        weight_kernel,
        grid=(hidden // TILE,),
        out_shape=[
            jax.ShapeDtypeStruct((feats, hidden), BF16),
            jax.ShapeDtypeStruct((hidden, feats), BF16),
        ],
        in_specs=[
            pl.BlockSpec((rows, feats), whole_block),
            pl.BlockSpec((rows, feats), whole_block),
            pl.BlockSpec((rows, TILE), lambda i: (0, i)),
            pl.BlockSpec((rows, TILE), lambda i: (0, i)),
        ],
        out_specs=[
            pl.BlockSpec((feats, TILE), lambda i: (0, i)),
            pl.BlockSpec((TILE, feats), lambda i: (i, 0)),
        ],
        compiler_params=pltpu.CompilerParams(vmem_limit_bytes=32 * 2**20),
        cost_estimate=pl.CostEstimate(
            flops=4 * rows * feats * hidden, bytes_accessed=4 * feats * hidden, transcendentals=0
        ),
    )(
        tok.reshape(rows, feats), og.reshape(rows, feats), act.reshape(rows, hidden), hg.reshape(rows, hidden)
    )
    return block_out, tokens_grad, w_in_grad, w_out_grad, bias_grad.reshape(-1)


def by_shape(mesh):
    def run(tokens, out_grad, w_in, b_in, w_out):
        depth_count = mesh.shape["depth"]
        fits = (
            mesh.shape["row"] == 4
            and depth_count == 2
            and mesh.shape["col"] % 2 == 0
            and tokens.shape[0] % 16 == 0
            and tokens.shape[1] % TILE == 0
            and w_in.shape[1] % (depth_count * TILE) == 0
        )
        if fits:
            return fused(mesh.shape["col"], tokens, out_grad, w_in, b_in, w_out)
        return local(tokens, out_grad, w_in, b_in, w_out)

    return run


def solution(mesh):
    return jax.shard_map(
        by_shape(mesh),
        mesh=mesh,
        in_specs=(
            P(("col", "depth"), "row"),
            P(("col", "depth"), "row"),
            P("row", "col"),
            P("col"),
            P("col", "row"),
        ),
        out_specs=(
            P(("col", "depth"), "row"),
            P(("col", "depth"), "row"),
            P("row", ("col", "depth")),
            P(("col", "depth"), "row"),
            P("col"),
        ),
        check_vma=False,
    )
```

```python
import functools

import jax
import jax.numpy as jnp
from jax import lax
from jax.experimental import pallas as pl
from jax.experimental.pallas import tpu as pltpu
from jax.sharding import PartitionSpec as P

root_coeff = 0.7978845608028654
cubic_coeff = 0.044715


def gelu_parts(pre_act):
    inner_arg = root_coeff * (pre_act + cubic_coeff * pre_act * pre_act * pre_act)
    tangent = jnp.tanh(inner_arg)
    gelu_value = 0.5 * pre_act * (1.0 + tangent)
    gelu_slope = 0.5 * (1.0 + tangent) + 0.5 * pre_act * (1.0 - tangent * tangent) * root_coeff * (
        1.0 + 3.0 * cubic_coeff * pre_act * pre_act
    )
    return (gelu_value, gelu_slope)


def right_transposed(left_side, right_side):
    return lax.dot_general(
        left_side, right_side, (((1,), (1,)), ((), ())), preferred_element_type=jnp.float32
    )


def left_transposed(left_side, right_side):
    return lax.dot_general(
        left_side, right_side, (((0,), (0,)), ((), ())), preferred_element_type=jnp.float32
    )


def depth_rows(gathered, col_count, depth_index, depth_count):
    tile_rows = gathered.shape[0] // (col_count * depth_count)
    shaped = gathered.reshape(col_count, depth_count, tile_rows, gathered.shape[1])
    picked = lax.dynamic_index_in_dim(shaped, depth_index, 1, keepdims=False)
    return picked.reshape(col_count * tile_rows, gathered.shape[1])


def local(tokens, out_grad, w_in, b_in, w_out):
    col_count = lax.axis_size("col")
    depth_count = lax.axis_size("depth")
    tile_rows = tokens.shape[0]
    part_cols = w_in.shape[1] // depth_count
    depth_index = lax.axis_index("depth")
    all_input, all_grad = (
        lax.all_gather(tokens, ("col", "depth"), axis=0, tiled=True),
        lax.all_gather(out_grad, ("col", "depth"), axis=0, tiled=True),
    )
    plane_input = depth_rows(all_input, col_count, depth_index, depth_count)
    plane_grad = depth_rows(all_grad, col_count, depth_index, depth_count)
    pre_sum = lax.psum_scatter(
        jnp.dot(plane_input, w_in, preferred_element_type=jnp.float32),
        "row",
        scatter_dimension=0,
        tiled=True,
    )
    pre_share = pre_sum + b_in
    gelu_value, gelu_slope = gelu_parts(pre_share)
    plane_act = lax.all_gather(gelu_value.astype(jnp.bfloat16), "row", axis=0, tiled=True)
    block_out = lax.psum_scatter(
        jnp.dot(plane_act, w_out, preferred_element_type=jnp.float32),
        "col",
        scatter_dimension=0,
        tiled=True,
    ).astype(jnp.bfloat16)
    grad_share = lax.psum_scatter(
        right_transposed(plane_grad, w_out), "row", scatter_dimension=0, tiled=True
    )
    pre_grad = grad_share * gelu_slope
    plane_hgrad = lax.all_gather(pre_grad.astype(jnp.bfloat16), "row", axis=0, tiled=True)
    b_in_grad = lax.psum(jnp.sum(pre_grad, axis=0), ("row", "depth"))
    tokens_grad = lax.psum_scatter(
        right_transposed(plane_hgrad, w_in), "col", scatter_dimension=0, tiled=True
    ).astype(jnp.bfloat16)
    act_parts = lax.all_to_all(
        plane_act.reshape(col_count, tile_rows, w_in.shape[1]),
        "depth",
        split_axis=2,
        concat_axis=1,
        tiled=True,
    )
    act_parts = act_parts.reshape(-1, part_cols)
    hgrad_parts = lax.all_to_all(
        plane_hgrad.reshape(col_count, tile_rows, w_in.shape[1]),
        "depth",
        split_axis=2,
        concat_axis=1,
        tiled=True,
    )
    hgrad_parts = hgrad_parts.reshape(-1, part_cols)
    w_in_grad = left_transposed(all_input, hgrad_parts)
    w_out_grad = left_transposed(act_parts, all_grad)
    return (
        block_out,
        tokens_grad,
        w_in_grad.astype(jnp.bfloat16),
        w_out_grad.astype(jnp.bfloat16),
        b_in_grad,
    )


MESH = pl.DeviceIdType.MESH
TILE = 256
BF16 = jnp.bfloat16
F32 = jnp.float32


def block_kernel(
    col_count,
    tokens_ref, grad_ref, w_in_ref, bias_ref, w_out_ref,
    out_ref, tgrad_ref, bgrad_ref, tok_out, og_out, act_out, hg_out,
    tok, og, w_in, w_out, part, core_in, chip16, y_in, act, hg, slope,
    x_out, x_in, z_sum, z_out, z_in, b_acc, b_core, b_own, b_x,
    local_sem, z_ssem, z_rsem, x_ssem, x_rsem, c_ssem, c_rsem, y_ssem, y_rsem,
    a_ssem, a_rsem, rx_ssem, rx_rsem, rz_ssem, rz_rsem, b_ssem, b_rsem, out_sem,
):
    row = lax.axis_index("row")
    col = lax.axis_index("col")
    depth = lax.axis_index("depth")
    core = lax.rem(row, 2)
    core_peer = {"row": row + 1 - 2 * core}
    y_peer = {"row": lax.rem(row + 2, 4)}
    x_peer = {"depth": 1 - depth}
    hidden = w_in.shape[1]
    feats = w_in.shape[0]
    half = part.shape[4]

    def z_peer(step):
        return {"col": lax.rem(col + step, col_count)}

    def remote(src, dst, ssem, rsem, peer):
        return pltpu.make_async_remote_copy(
            src_ref=src, dst_ref=dst, send_sem=ssem, recv_sem=rsem, device_id=peer, device_id_type=MESH
        )

    base = pl.multiple_of(depth * hidden, 128)
    locals_ = [
        pltpu.make_async_copy(tokens_ref, tok.at[0, 0], local_sem.at[0]),
        pltpu.make_async_copy(w_in_ref.at[:, pl.ds(base, hidden)], w_in, local_sem.at[1]),
        pltpu.make_async_copy(grad_ref, og.at[0, 0], local_sem.at[2]),
        pltpu.make_async_copy(w_out_ref.at[pl.ds(base, hidden), :], w_out, local_sem.at[3]),
    ]
    for copy in locals_:
        copy.start()

    barrier = pltpu.get_barrier_semaphore()
    peers = [z_peer(step) for step in range(1, col_count)] + [x_peer, y_peer, core_peer]
    for peer in peers:
        pl.semaphore_signal(barrier, inc=1, device_id=peer, device_id_type=MESH)
    pl.semaphore_wait(barrier, len(peers))

    sends = []

    def start(copy):
        copy.start()
        sends.append(copy)
        return copy

    def gather_start(which, src, dst):
        start(remote(src, dst.at[1, 0], x_ssem.at[which, 0], x_rsem.at[which, 0], x_peer))
        for step in range(1, col_count):
            start(remote(src, dst.at[0, step], z_ssem.at[which, step], z_rsem.at[which, step], z_peer(step)))

    def gather_own(which, dst):
        for step in range(1, col_count):
            block = dst.at[0, step]
            remote(block, block, z_ssem.at[which, step], z_rsem.at[which, step], z_peer(step)).wait_recv()
            start(remote(block, dst.at[1, step], x_ssem.at[which, step], x_rsem.at[which, step], x_peer))

    def gather_other(which, dst):
        for step in range(col_count):
            block = dst.at[1, step]
            remote(block, block, x_ssem.at[which, step], x_rsem.at[which, step], x_peer).wait_recv()

    def tile_of(i):
        return pl.ds(pl.multiple_of(i * TILE, TILE), TILE)

    def rows_of(buf, group):
        chunk, first, count = group
        value = buf[chunk, first:first + count]
        return value.reshape(-1, value.shape[-1])

    def slots(buf, group, *before):
        chunk, first, count = group
        return buf.at[(*before, chunk, pl.ds(first, count))]

    def sem_of(group):
        return group[0], min(group[1], 1)

    def product(which, group, multiply):
        chunk, first, count = group

        @pl.loop(0, hidden // TILE)
        def _(i):
            at = tile_of(i)
            value = multiply(rows_of(og if which else tok, group), at)
            for n in range(2 * count):
                part[which, chunk, n % 2, first + n // 2, :, at] = value[n * half:(n + 1) * half]

        start(remote(
            part.at[which, chunk, 1 - core, pl.ds(first, count)], slots(core_in, group, which),
            c_ssem.at[(which, *sem_of(group))], c_rsem.at[(which, *sem_of(group))], core_peer,
        ))

    def chip_sum(which, group):
        chunk, first, count = group
        landed = slots(core_in, group, which)
        remote(
            landed, landed, c_ssem.at[(which, *sem_of(group))], c_rsem.at[(which, *sem_of(group))], core_peer
        ).wait_recv()

        @pl.loop(0, hidden // TILE)
        def _(i):
            at = tile_of(i)
            for s in range(first, first + count):
                total = part[which, chunk, core, s, :, at] + core_in[which, chunk, s, :, at]
                chip16[which, chunk, s, :, at] = total.astype(BF16)

        start(remote(
            slots(chip16, group, which), slots(y_in, group, which),
            y_ssem.at[(which, *sem_of(group))], y_rsem.at[(which, *sem_of(group))], y_peer,
        ))

    def y_wait(which, group):
        landed = slots(y_in, group, which)
        remote(
            landed, landed, y_ssem.at[(which, *sem_of(group))], y_rsem.at[(which, *sem_of(group))], y_peer
        ).wait_recv()

    def row_sum(which, chunk, s, at):
        return chip16[which, chunk, s, :, at].astype(F32) + y_in[which, chunk, s, :, at].astype(F32)

    def share(which, group, buf, whose):
        chunk, first, count = group
        piece = buf.at[chunk, pl.ds(first, count), whose]
        return remote(
            piece, piece, a_ssem.at[(which, *sem_of(group))], a_rsem.at[(which, *sem_of(group))], core_peer
        )

    def activate(group):
        chunk, first, count = group
        y_wait(0, group)

        @pl.loop(0, hidden // TILE)
        def _(i):
            at = tile_of(i)
            bias = bias_ref[:, pl.ds(pl.multiple_of(depth * hidden + i * TILE, 128), TILE)]
            for s in range(first, first + count):
                value, slope_here = gelu_parts(row_sum(0, chunk, s, at) + bias)
                act[chunk, s, core, :, at] = value.astype(BF16)
                slope[chunk, s, :, at] = slope_here

        start(share(0, group, act, core))

    def hidden_grad(group, fresh):
        chunk, first, count = group
        y_wait(1, group)

        @pl.loop(0, hidden // TILE)
        def _(i):
            at = tile_of(i)
            total = None if fresh else b_acc[:, at]
            for s in range(first, first + count):
                pre_grad = row_sum(1, chunk, s, at) * slope[chunk, s, :, at]
                hg[chunk, s, core, :, at] = pre_grad.astype(BF16)
                here = jnp.sum(pre_grad, axis=0, keepdims=True)
                total = here if total is None else total + here
            b_acc[:, at] = total

        start(share(1, group, hg, core))

    def project(which, chunk, buf, multiply):
        tile_rows = x_out.shape[2]

        @pl.loop(0, feats // TILE)
        def _(i):
            at = tile_of(i)
            value = multiply(rows_of(buf, (chunk, 0, col_count)), at)
            for c in range(col_count):
                piece = value[c * tile_rows:(c + 1) * tile_rows]
                if chunk == 1:
                    x_out[which, c, :, at] = piece.astype(BF16)
                else:
                    z_sum[which, c, :, at] = piece

        if chunk == 1:
            start(remote(x_out.at[which], x_in.at[which], rx_ssem.at[which], rx_rsem.at[which], x_peer))

    def plane_sum(which):
        landed = x_in.at[which]
        remote(landed, landed, rx_ssem.at[which], rx_rsem.at[which], x_peer).wait_recv()
        for c in range(col_count):
            total = z_sum[which, c] + x_in[which, c].astype(F32)
            z_sum[which, c] = total
            z_out[which, c] = total.astype(BF16)
        for step in range(1, col_count):
            start(remote(
                z_out.at[which, col_count - step], z_in.at[which, step - 1],
                rz_ssem.at[which, step - 1], rz_rsem.at[which, step - 1], z_peer(step),
            ))

    def final_sum(which, result):
        for step in range(1, col_count):
            landed = z_in.at[which, step - 1]
            remote(
                landed, landed, rz_ssem.at[which, step - 1], rz_rsem.at[which, step - 1], z_peer(step)
            ).wait_recv()
        total = z_sum[which, 0]
        for step in range(1, col_count):
            total = total + z_in[which, step - 1].astype(F32)
        result[...] = total.astype(BF16)

    def keep(which, src, dst):
        copy = pltpu.make_async_copy(src, dst, out_sem.at[which])
        copy.start()
        return copy

    def pre_tile(value, at):
        return jnp.dot(value, w_in[:, at], preferred_element_type=F32)

    def back_tile(value, at):
        return right_transposed(value, w_out[at, :])

    own, rest, other = (0, 0, 1), (0, 1, col_count - 1), (1, 0, col_count)

    gather_start(0, tokens_ref, tok)
    locals_[0].wait()
    locals_[1].wait()
    product(0, own, pre_tile)
    locals_[2].wait()
    locals_[3].wait()
    product(1, own, back_tile)
    chip_sum(0, own)
    gather_own(0, tok)
    gather_start(1, grad_ref, og)
    chip_sum(1, own)
    product(0, rest, pre_tile)
    chip_sum(0, rest)
    gather_other(0, tok)
    kept = [keep(0, tok, tok_out)]
    product(0, other, pre_tile)
    chip_sum(0, other)
    gather_own(1, og)
    activate(own)
    gather_other(1, og)
    kept.append(keep(1, og, og_out))
    product(1, other, back_tile)
    chip_sum(1, other)
    product(1, rest, back_tile)
    chip_sum(1, rest)
    activate(rest)
    activate(other)
    for group in (own, rest, other):
        share(0, group, act, 1 - core).wait_recv()
    kept.append(keep(2, act, act_out))

    def forward(value, at):
        return jnp.dot(value, w_out[:, at], preferred_element_type=F32)

    def backward(value, at):
        return right_transposed(value, w_in[at, :])

    project(0, 1, act, forward)
    project(0, 0, act, forward)
    plane_sum(0)
    hidden_grad(own, True)
    hidden_grad(other, False)
    share(1, own, hg, 1 - core).wait_recv()
    share(1, other, hg, 1 - core).wait_recv()
    project(1, 1, hg, backward)
    hidden_grad(rest, False)
    start(remote(b_acc, b_core, b_ssem.at[0], b_rsem.at[0], core_peer))
    share(1, rest, hg, 1 - core).wait_recv()
    kept.append(keep(3, hg, hg_out))
    project(1, 0, hg, backward)
    plane_sum(1)
    remote(b_core, b_core, b_ssem.at[0], b_rsem.at[0], core_peer).wait_recv()
    b_own[...] = b_acc[...] + b_core[...]
    start(remote(b_own, b_x, b_ssem.at[1], b_rsem.at[1], x_peer))
    final_sum(0, out_ref)
    remote(b_x, b_x, b_ssem.at[1], b_rsem.at[1], x_peer).wait_recv()
    bgrad_ref[:, pl.ds(base, hidden)] = b_own[...]
    bgrad_ref[:, pl.ds(pl.multiple_of((1 - depth) * hidden, 128), hidden)] = b_x[...]
    final_sum(1, tgrad_ref)
    for copy in kept:
        copy.wait()
    for copy in sends:
        copy.wait_send()


def weight_kernel(
    tok_ref, og_ref, act_ref, hg_ref, out_ref, tgrad_ref,
    w_in_grad_ref, w_out_grad_ref, out_again, tgrad_again, tok_turned,
):
    @pl.when(pl.program_id(0) == 0)
    def _():
        tok_turned[...] = tok_ref[...].T
        out_again[...] = out_ref[...]
        tgrad_again[...] = tgrad_ref[...]

    w_in_grad_ref[...] = jnp.dot(tok_turned[...], hg_ref[...], preferred_element_type=F32).astype(BF16)
    w_out_grad_ref[...] = left_transposed(act_ref[...], og_ref[...]).astype(BF16)


def fused(col_count, tokens, out_grad, w_in, b_in, w_out):
    tile_rows, feats = tokens.shape
    hidden = w_in.shape[1] // 2
    plane = col_count * tile_rows
    half = tile_rows // 2
    rows = 2 * plane
    anywhere = pl.BlockSpec(memory_space=pltpu.HBM)
    vmem = pl.BlockSpec(memory_space=pltpu.VMEM)
    dma = pltpu.SemaphoreType.DMA
    outs = pl.pallas_call(
        functools.partial(block_kernel, col_count),
        out_shape=[
            jax.ShapeDtypeStruct((tile_rows, feats), BF16),
            jax.ShapeDtypeStruct((tile_rows, feats), BF16),
            jax.ShapeDtypeStruct((1, 2 * hidden), F32),
            jax.ShapeDtypeStruct((2, col_count, tile_rows, feats), BF16),
            jax.ShapeDtypeStruct((2, col_count, tile_rows, feats), BF16),
            jax.ShapeDtypeStruct((2, col_count, 2, half, hidden), BF16),
            jax.ShapeDtypeStruct((2, col_count, 2, half, hidden), BF16),
        ],
        in_specs=[anywhere, anywhere, anywhere, vmem, anywhere],
        out_specs=[vmem, vmem, vmem, anywhere, anywhere, anywhere, anywhere],
        scratch_shapes=[
            pltpu.VMEM((2, col_count, tile_rows, feats), BF16),
            pltpu.VMEM((2, col_count, tile_rows, feats), BF16),
            pltpu.VMEM((feats, hidden), BF16),
            pltpu.VMEM((hidden, feats), BF16),
            pltpu.VMEM((2, 2, 2, col_count, half, hidden), F32),
            pltpu.VMEM((2, 2, col_count, half, hidden), F32),
            pltpu.VMEM((2, 2, col_count, half, hidden), BF16),
            pltpu.VMEM((2, 2, col_count, half, hidden), BF16),
            pltpu.VMEM((2, col_count, 2, half, hidden), BF16),
            pltpu.VMEM((2, col_count, 2, half, hidden), BF16),
            pltpu.VMEM((2, col_count, half, hidden), F32),
            pltpu.VMEM((2, col_count, tile_rows, feats), BF16),
            pltpu.VMEM((2, col_count, tile_rows, feats), BF16),
            pltpu.VMEM((2, col_count, tile_rows, feats), F32),
            pltpu.VMEM((2, col_count, tile_rows, feats), BF16),
            pltpu.VMEM((2, col_count - 1, tile_rows, feats), BF16),
            pltpu.VMEM((1, hidden), F32),
            pltpu.VMEM((1, hidden), F32),
            pltpu.VMEM((1, hidden), F32),
            pltpu.VMEM((1, hidden), F32),
            dma((4,)),
            dma((2, col_count)),
            dma((2, col_count)),
            dma((2, col_count)),
            dma((2, col_count)),
            dma((2, 2, 2)),
            dma((2, 2, 2)),
            dma((2, 2, 2)),
            dma((2, 2, 2)),
            dma((2, 2, 2)),
            dma((2, 2, 2)),
            dma((2,)),
            dma((2,)),
            dma((2, col_count - 1)),
            dma((2, col_count - 1)),
            dma((2,)),
            dma((2,)),
            dma((4,)),
        ],
        compiler_params=pltpu.CompilerParams(
            collective_id=0, has_side_effects=True, vmem_limit_bytes=44 * 2**20
        ),
        cost_estimate=pl.CostEstimate(
            flops=8 * rows * feats * hidden, bytes_accessed=8 * feats * hidden, transcendentals=rows * hidden
        ),
    )(tokens, out_grad, w_in, b_in.reshape(1, -1), w_out)
    block_out, tokens_grad, bias_grad, tok, og, act, hg = outs
    whole_block = lambda i: (0, 0)
    w_in_grad, w_out_grad, block_out, tokens_grad = pl.pallas_call(
        weight_kernel,
        grid=(hidden // TILE,),
        out_shape=[
            jax.ShapeDtypeStruct((feats, hidden), BF16),
            jax.ShapeDtypeStruct((hidden, feats), BF16),
            jax.ShapeDtypeStruct((tile_rows, feats), BF16),
            jax.ShapeDtypeStruct((tile_rows, feats), BF16),
        ],
        in_specs=[
            pl.BlockSpec((rows, feats), whole_block),
            pl.BlockSpec((rows, feats), whole_block),
            pl.BlockSpec((rows, TILE), lambda i: (0, i)),
            pl.BlockSpec((rows, TILE), lambda i: (0, i)),
            pl.BlockSpec((tile_rows, feats), whole_block),
            pl.BlockSpec((tile_rows, feats), whole_block),
        ],
        out_specs=[
            pl.BlockSpec((feats, TILE), lambda i: (0, i)),
            pl.BlockSpec((TILE, feats), lambda i: (i, 0)),
            pl.BlockSpec((tile_rows, feats), whole_block),
            pl.BlockSpec((tile_rows, feats), whole_block),
        ],
        scratch_shapes=[pltpu.VMEM((feats, rows), BF16)],
        compiler_params=pltpu.CompilerParams(vmem_limit_bytes=32 * 2**20),
        cost_estimate=pl.CostEstimate(
            flops=4 * rows * feats * hidden, bytes_accessed=4 * feats * hidden, transcendentals=0
        ),
    )(
        tok.reshape(rows, feats), og.reshape(rows, feats), act.reshape(rows, hidden), hg.reshape(rows, hidden),
        block_out, tokens_grad,
    )
    return block_out, tokens_grad, w_in_grad, w_out_grad, bias_grad.reshape(-1)


def by_shape(mesh):
    def run(tokens, out_grad, w_in, b_in, w_out):
        depth_count = mesh.shape["depth"]
        fits = (
            mesh.shape["row"] == 4
            and depth_count == 2
            and mesh.shape["col"] > 1
            and tokens.shape[0] % 32 == 0
            and tokens.shape[1] % TILE == 0
            and w_in.shape[1] % (depth_count * TILE) == 0
        )
        if fits:
            return fused(mesh.shape["col"], tokens, out_grad, w_in, b_in, w_out)
        return local(tokens, out_grad, w_in, b_in, w_out)

    return run


def solution(mesh):
    return jax.shard_map(
        by_shape(mesh),
        mesh=mesh,
        in_specs=(
            P(("col", "depth"), "row"),
            P(("col", "depth"), "row"),
            P("row", "col"),
            P("col"),
            P("col", "row"),
        ),
        out_specs=(
            P(("col", "depth"), "row"),
            P(("col", "depth"), "row"),
            P("row", ("col", "depth")),
            P(("col", "depth"), "row"),
            P("col"),
        ),
        check_vma=False,
    )
```

```python
import functools

import jax
import jax.numpy as jnp
from jax import lax
from jax.experimental import pallas as pl
from jax.experimental.pallas import tpu as pltpu
from jax.sharding import PartitionSpec as P

root_coeff = 0.7978845608028654
cubic_coeff = 0.044715


def gelu_parts(pre_act):
    inner_arg = root_coeff * (pre_act + cubic_coeff * pre_act * pre_act * pre_act)
    tangent = jnp.tanh(inner_arg)
    gelu_value = 0.5 * pre_act * (1.0 + tangent)
    gelu_slope = 0.5 * (1.0 + tangent) + 0.5 * pre_act * (1.0 - tangent * tangent) * root_coeff * (
        1.0 + 3.0 * cubic_coeff * pre_act * pre_act
    )
    return (gelu_value, gelu_slope)


def right_transposed(left_side, right_side):
    return lax.dot_general(
        left_side, right_side, (((1,), (1,)), ((), ())), preferred_element_type=jnp.float32
    )


def left_transposed(left_side, right_side):
    return lax.dot_general(
        left_side, right_side, (((0,), (0,)), ((), ())), preferred_element_type=jnp.float32
    )


def depth_rows(gathered, col_count, depth_index, depth_count):
    tile_rows = gathered.shape[0] // (col_count * depth_count)
    shaped = gathered.reshape(col_count, depth_count, tile_rows, gathered.shape[1])
    picked = lax.dynamic_index_in_dim(shaped, depth_index, 1, keepdims=False)
    return picked.reshape(col_count * tile_rows, gathered.shape[1])


def local(tokens, out_grad, w_in, b_in, w_out):
    col_count = lax.axis_size("col")
    depth_count = lax.axis_size("depth")
    tile_rows = tokens.shape[0]
    part_cols = w_in.shape[1] // depth_count
    depth_index = lax.axis_index("depth")
    all_input, all_grad = (
        lax.all_gather(tokens, ("col", "depth"), axis=0, tiled=True),
        lax.all_gather(out_grad, ("col", "depth"), axis=0, tiled=True),
    )
    plane_input = depth_rows(all_input, col_count, depth_index, depth_count)
    plane_grad = depth_rows(all_grad, col_count, depth_index, depth_count)
    pre_sum = lax.psum_scatter(
        jnp.dot(plane_input, w_in, preferred_element_type=jnp.float32),
        "row",
        scatter_dimension=0,
        tiled=True,
    )
    pre_share = pre_sum + b_in
    gelu_value, gelu_slope = gelu_parts(pre_share)
    plane_act = lax.all_gather(gelu_value.astype(jnp.bfloat16), "row", axis=0, tiled=True)
    block_out = lax.psum_scatter(
        jnp.dot(plane_act, w_out, preferred_element_type=jnp.float32),
        "col",
        scatter_dimension=0,
        tiled=True,
    ).astype(jnp.bfloat16)
    grad_share = lax.psum_scatter(
        right_transposed(plane_grad, w_out), "row", scatter_dimension=0, tiled=True
    )
    pre_grad = grad_share * gelu_slope
    plane_hgrad = lax.all_gather(pre_grad.astype(jnp.bfloat16), "row", axis=0, tiled=True)
    b_in_grad = lax.psum(jnp.sum(pre_grad, axis=0), ("row", "depth"))
    tokens_grad = lax.psum_scatter(
        right_transposed(plane_hgrad, w_in), "col", scatter_dimension=0, tiled=True
    ).astype(jnp.bfloat16)
    act_parts = lax.all_to_all(
        plane_act.reshape(col_count, tile_rows, w_in.shape[1]),
        "depth",
        split_axis=2,
        concat_axis=1,
        tiled=True,
    )
    act_parts = act_parts.reshape(-1, part_cols)
    hgrad_parts = lax.all_to_all(
        plane_hgrad.reshape(col_count, tile_rows, w_in.shape[1]),
        "depth",
        split_axis=2,
        concat_axis=1,
        tiled=True,
    )
    hgrad_parts = hgrad_parts.reshape(-1, part_cols)
    w_in_grad = left_transposed(all_input, hgrad_parts)
    w_out_grad = left_transposed(act_parts, all_grad)
    return (
        block_out,
        tokens_grad,
        w_in_grad.astype(jnp.bfloat16),
        w_out_grad.astype(jnp.bfloat16),
        b_in_grad,
    )


MESH = pl.DeviceIdType.MESH
TILE = 256
BF16 = jnp.bfloat16
F32 = jnp.float32


def block_kernel(
    col_count,
    tokens_ref, grad_ref, w_in_ref, bias_ref, w_out_ref,
    *refs,
):
    away = col_count - 1
    out_ref, tgrad_ref, bgrad_ref, tok_out, og_out, act_out, hg_out = refs[:7]
    tgrad_away = refs[7:7 + away]
    (
    tok, og, w_in, w_out, bias, b_all, part, part16, core_in, chip16, y_in, act, hg, slope,
    x_out, x_in, z_sum, z_out, z_in, b_acc, b_core, b_own, b_x,
    local_sem, z_ssem, z_rsem, x_ssem, x_rsem, c_ssem, c_rsem, y_ssem, y_rsem,
    a_ssem, a_rsem, rx_ssem, rx_rsem, rz_ssem, rz_rsem, b_ssem, b_rsem, out_sem,
    ) = refs[7 + away:]
    row = lax.axis_index("row")
    col = lax.axis_index("col")
    depth = lax.axis_index("depth")
    core = lax.rem(row, 2)
    core_peer = {"row": row + 1 - 2 * core}
    y_peer = {"row": lax.rem(row + 2, 4)}
    x_peer = {"depth": 1 - depth}
    hidden = w_in.shape[1]
    feats = w_in.shape[0]
    half = part.shape[4]

    def z_peer(step):
        return {"col": lax.rem(col + step, col_count)}

    def remote(src, dst, ssem, rsem, peer):
        return pltpu.make_async_remote_copy(
            src_ref=src, dst_ref=dst, send_sem=ssem, recv_sem=rsem, device_id=peer, device_id_type=MESH
        )

    base = pl.multiple_of(depth * hidden, 128)
    locals_ = [
        pltpu.make_async_copy(tokens_ref, tok.at[0, 0], local_sem.at[0]),
        pltpu.make_async_copy(w_in_ref.at[:, pl.ds(base, hidden)], w_in, local_sem.at[1]),
        pltpu.make_async_copy(grad_ref, og.at[0, 0], local_sem.at[2]),
        pltpu.make_async_copy(w_out_ref.at[pl.ds(base, hidden), :], w_out, local_sem.at[3]),
        pltpu.make_async_copy(bias_ref, bias, local_sem.at[4]),
    ]
    for copy in locals_:
        copy.start()

    barrier = pltpu.get_barrier_semaphore()
    peers = [z_peer(step) for step in range(1, col_count)] + [x_peer, y_peer, core_peer]
    for peer in peers:
        pl.semaphore_signal(barrier, inc=1, device_id=peer, device_id_type=MESH)
    pl.semaphore_wait(barrier, len(peers))

    sends = []

    def start(copy):
        copy.start()
        sends.append(copy)
        return copy

    def gather_start(which, src, dst):
        start(remote(src, dst.at[1, 0], x_ssem.at[which, 0], x_rsem.at[which, 0], x_peer))
        for step in range(1, col_count):
            start(remote(src, dst.at[0, step], z_ssem.at[which, step], z_rsem.at[which, step], z_peer(step)))

    def gather_own(which, dst):
        for step in range(1, col_count):
            block = dst.at[0, step]
            remote(block, block, z_ssem.at[which, step], z_rsem.at[which, step], z_peer(step)).wait_recv()
            start(remote(block, dst.at[1, step], x_ssem.at[which, step], x_rsem.at[which, step], x_peer))

    def gather_other(which, dst):
        for step in range(col_count):
            block = dst.at[1, step]
            remote(block, block, x_ssem.at[which, step], x_rsem.at[which, step], x_peer).wait_recv()

    def tile_of(i):
        return pl.ds(pl.multiple_of(i * TILE, TILE), TILE)

    def rows_of(buf, group):
        chunk, first, count = group
        value = buf[chunk, first:first + count]
        return value.reshape(-1, value.shape[-1])

    def slots(buf, group, *before):
        chunk, first, count = group
        return buf.at[(*before, chunk, pl.ds(first, count))]

    def sem_of(group):
        return group[0], min(group[1], 1)

    def product(which, group, multiply):
        chunk, first, count = group

        @pl.loop(0, hidden // TILE)
        def _(i):
            at = tile_of(i)
            value = multiply(rows_of(og if which else tok, group), at)
            for n in range(2 * count):
                piece = value[n * half:(n + 1) * half]
                part[which, chunk, n % 2, first + n // 2, :, at] = piece
                part16[which, chunk, n % 2, first + n // 2, :, at] = piece.astype(BF16)

        start(remote(
            part16.at[which, chunk, 1 - core, pl.ds(first, count)], slots(core_in, group, which),
            c_ssem.at[(which, *sem_of(group))], c_rsem.at[(which, *sem_of(group))], core_peer,
        ))

    def chip_sum(which, group):
        chunk, first, count = group
        landed = slots(core_in, group, which)
        remote(
            landed, landed, c_ssem.at[(which, *sem_of(group))], c_rsem.at[(which, *sem_of(group))], core_peer
        ).wait_recv()

        @pl.loop(0, hidden // TILE)
        def _(i):
            at = tile_of(i)
            for s in range(first, first + count):
                total = part[which, chunk, core, s, :, at] + core_in[which, chunk, s, :, at].astype(F32)
                chip16[which, chunk, s, :, at] = total.astype(BF16)

        start(remote(
            slots(chip16, group, which), slots(y_in, group, which),
            y_ssem.at[(which, *sem_of(group))], y_rsem.at[(which, *sem_of(group))], y_peer,
        ))

    def y_wait(which, group):
        landed = slots(y_in, group, which)
        remote(
            landed, landed, y_ssem.at[(which, *sem_of(group))], y_rsem.at[(which, *sem_of(group))], y_peer
        ).wait_recv()

    def row_sum(which, chunk, s, at):
        return chip16[which, chunk, s, :, at].astype(F32) + y_in[which, chunk, s, :, at].astype(F32)

    def share(which, group, buf, whose):
        chunk, first, count = group
        piece = buf.at[chunk, pl.ds(first, count), whose]
        return remote(
            piece, piece, a_ssem.at[(which, *sem_of(group))], a_rsem.at[(which, *sem_of(group))], core_peer
        )

    def activate(group):
        chunk, first, count = group
        y_wait(0, group)

        @pl.loop(0, hidden // TILE)
        def _(i):
            at = tile_of(i)
            bias_here = b_all[:, pl.ds(pl.multiple_of(depth * hidden + i * TILE, 128), TILE)]
            for s in range(first, first + count):
                value, slope_here = gelu_parts(row_sum(0, chunk, s, at) + bias_here)
                act[chunk, s, core, :, at] = value.astype(BF16)
                slope[chunk, s, :, at] = slope_here

        start(share(0, group, act, core))

    def hidden_grad(group, fresh):
        chunk, first, count = group
        y_wait(1, group)

        @pl.loop(0, hidden // TILE)
        def _(i):
            at = tile_of(i)
            total = None if fresh else b_acc[:, at]
            for s in range(first, first + count):
                pre_grad = row_sum(1, chunk, s, at) * slope[chunk, s, :, at]
                hg[chunk, s, core, :, at] = pre_grad.astype(BF16)
                here = jnp.sum(pre_grad, axis=0, keepdims=True)
                total = here if total is None else total + here
            b_acc[:, at] = total

        start(share(1, group, hg, core))

    def project(which, chunk, buf, multiply):
        tile_rows = x_out.shape[2]

        @pl.loop(0, feats // TILE)
        def _(i):
            at = tile_of(i)
            value = multiply(rows_of(buf, (chunk, 0, col_count)), at)
            for c in range(col_count):
                piece = value[c * tile_rows:(c + 1) * tile_rows]
                if chunk == 1:
                    x_out[which, c, :, at] = piece.astype(BF16)
                else:
                    z_sum[which, c, :, at] = piece

        if chunk == 1:
            start(remote(x_out.at[which], x_in.at[which], rx_ssem.at[which], rx_rsem.at[which], x_peer))

    def plane_sum(which):
        landed = x_in.at[which]
        remote(landed, landed, rx_ssem.at[which], rx_rsem.at[which], x_peer).wait_recv()
        for c in range(col_count):
            total = z_sum[which, c] + x_in[which, c].astype(F32)
            z_sum[which, c] = total
            z_out[which, c] = total.astype(BF16)
        for step in range(1, col_count):
            start(remote(
                z_out.at[which, col_count - step], z_in.at[which, step - 1],
                rz_ssem.at[which, step - 1], rz_rsem.at[which, step - 1], z_peer(step),
            ))

    def final_sum(which, result):
        for step in range(1, col_count):
            landed = z_in.at[which, step - 1]
            remote(
                landed, landed, rz_ssem.at[which, step - 1], rz_rsem.at[which, step - 1], z_peer(step)
            ).wait_recv()
        total = z_sum[which, 0]
        for step in range(1, col_count):
            total = total + z_in[which, step - 1].astype(F32)
        result[...] = total.astype(BF16)

    def keep(which, src, dst):
        copy = pltpu.make_async_copy(src, dst, out_sem.at[which])
        copy.start()
        return copy

    def pre_tile(value, at):
        return jnp.dot(value, w_in[:, at], preferred_element_type=F32)

    def back_tile(value, at):
        return right_transposed(value, w_out[at, :])

    near, far = (0, 0, col_count), (1, 0, col_count)

    gather_start(0, tokens_ref, tok)
    locals_[4].wait()
    b_all[...] = bias[...].reshape(1, 2 * hidden)
    locals_[0].wait()
    locals_[1].wait()
    gather_own(0, tok)
    gather_start(1, grad_ref, og)
    product(0, near, pre_tile)
    gather_other(0, tok)
    chip_sum(0, near)
    product(0, far, pre_tile)
    kept = [keep(0, tok, tok_out)]
    chip_sum(0, far)
    locals_[2].wait()
    locals_[3].wait()
    gather_own(1, og)
    product(1, near, back_tile)
    gather_other(1, og)
    kept.append(keep(1, og, og_out))
    product(1, far, back_tile)
    activate(near)
    chip_sum(1, far)
    chip_sum(1, near)
    activate(far)
    share(0, near, act, 1 - core).wait_recv()

    def forward(value, at):
        return jnp.dot(value, w_out[:, at], preferred_element_type=F32)

    def backward(value, at):
        return right_transposed(value, w_in[at, :])

    share(0, far, act, 1 - core).wait_recv()
    kept.append(keep(2, act, act_out))
    project(0, 1, act, forward)
    project(0, 0, act, forward)
    hidden_grad(far, True)
    share(1, far, hg, 1 - core).wait_recv()
    project(1, 1, hg, backward)
    plane_sum(0)
    hidden_grad(near, False)
    start(remote(b_acc, b_core, b_ssem.at[0], b_rsem.at[0], core_peer))
    share(1, near, hg, 1 - core).wait_recv()
    kept.append(keep(3, hg, hg_out))
    project(1, 0, hg, backward)
    remote(b_core, b_core, b_ssem.at[0], b_rsem.at[0], core_peer).wait_recv()
    b_own[...] = b_acc[...] + b_core[...]
    start(remote(b_own, b_x, b_ssem.at[1], b_rsem.at[1], x_peer))
    final_sum(0, out_ref)
    landed = x_in.at[1]
    remote(landed, landed, rx_ssem.at[1], rx_rsem.at[1], x_peer).wait_recv()
    tgrad_ref[...] = z_sum[1, 0] + x_in[1, 0].astype(F32)
    for step in range(1, col_count):
        total = z_sum[1, col_count - step] + x_in[1, col_count - step].astype(F32)
        tgrad_away[step - 1][...] = total.astype(BF16)
    remote(b_x, b_x, b_ssem.at[1], b_rsem.at[1], x_peer).wait_recv()
    b_all[:, pl.ds(base, hidden)] = b_own[...]
    b_all[:, pl.ds(pl.multiple_of((1 - depth) * hidden, 128), hidden)] = b_x[...]
    bgrad_ref[...] = b_all[...].reshape(2 * hidden)
    for copy in kept:
        copy.wait()
    for copy in sends:
        copy.wait_send()


def weight_kernel(
    tok_ref, og_ref, act_ref, hg_ref, out_ref, w_in_grad_ref, w_out_grad_ref, out_again, tok_turned,
):
    @pl.when(pl.program_id(0) == 0)
    def _():
        tok_turned[...] = tok_ref[...].T
        out_again[...] = out_ref[...]

    w_in_grad_ref[...] = jnp.dot(tok_turned[...], hg_ref[...], preferred_element_type=F32).astype(BF16)
    w_out_grad_ref[...] = left_transposed(act_ref[...], og_ref[...]).astype(BF16)


def fused(col_count, tokens, out_grad, w_in, b_in, w_out):
    tile_rows, feats = tokens.shape
    hidden = w_in.shape[1] // 2
    plane = col_count * tile_rows
    half = tile_rows // 2
    rows = 2 * plane
    anywhere = pl.BlockSpec(memory_space=pltpu.HBM)
    vmem = pl.BlockSpec(memory_space=pltpu.VMEM)
    dma = pltpu.SemaphoreType.DMA
    outs = pl.pallas_call(
        functools.partial(block_kernel, col_count),
        out_shape=[
            jax.ShapeDtypeStruct((tile_rows, feats), BF16),
            jax.ShapeDtypeStruct((tile_rows, feats), F32),
            jax.ShapeDtypeStruct((2 * hidden,), F32),
            jax.ShapeDtypeStruct((2, col_count, tile_rows, feats), BF16),
            jax.ShapeDtypeStruct((2, col_count, tile_rows, feats), BF16),
            jax.ShapeDtypeStruct((2, col_count, 2, half, hidden), BF16),
            jax.ShapeDtypeStruct((2, col_count, 2, half, hidden), BF16),
        ] + [jax.ShapeDtypeStruct((tile_rows, feats), BF16)] * (col_count - 1),
        in_specs=[anywhere] * 5,
        out_specs=[vmem, vmem, vmem, anywhere, anywhere, anywhere, anywhere] + [vmem] * (col_count - 1),
        scratch_shapes=[
            pltpu.VMEM((2, col_count, tile_rows, feats), BF16),
            pltpu.VMEM((2, col_count, tile_rows, feats), BF16),
            pltpu.VMEM((feats, hidden), BF16),
            pltpu.VMEM((hidden, feats), BF16),
            pltpu.VMEM((2 * hidden,), F32),
            pltpu.VMEM((1, 2 * hidden), F32),
            pltpu.VMEM((2, 2, 2, col_count, half, hidden), F32),
            pltpu.VMEM((2, 2, 2, col_count, half, hidden), BF16),
            pltpu.VMEM((2, 2, col_count, half, hidden), BF16),
            pltpu.VMEM((2, 2, col_count, half, hidden), BF16),
            pltpu.VMEM((2, 2, col_count, half, hidden), BF16),
            pltpu.VMEM((2, col_count, 2, half, hidden), BF16),
            pltpu.VMEM((2, col_count, 2, half, hidden), BF16),
            pltpu.VMEM((2, col_count, half, hidden), F32),
            pltpu.VMEM((2, col_count, tile_rows, feats), BF16),
            pltpu.VMEM((2, col_count, tile_rows, feats), BF16),
            pltpu.VMEM((2, col_count, tile_rows, feats), F32),
            pltpu.VMEM((2, col_count, tile_rows, feats), BF16),
            pltpu.VMEM((2, col_count - 1, tile_rows, feats), BF16),
            pltpu.VMEM((1, hidden), F32),
            pltpu.VMEM((1, hidden), F32),
            pltpu.VMEM((1, hidden), F32),
            pltpu.VMEM((1, hidden), F32),
            dma((5,)),
            dma((2, col_count)),
            dma((2, col_count)),
            dma((2, col_count)),
            dma((2, col_count)),
            dma((2, 2, 2)),
            dma((2, 2, 2)),
            dma((2, 2, 2)),
            dma((2, 2, 2)),
            dma((2, 2, 2)),
            dma((2, 2, 2)),
            dma((2,)),
            dma((2,)),
            dma((2, col_count - 1)),
            dma((2, col_count - 1)),
            dma((2,)),
            dma((2,)),
            dma((4,)),
        ],
        compiler_params=pltpu.CompilerParams(
            collective_id=0, has_side_effects=True, vmem_limit_bytes=44 * 2**20
        ),
        cost_estimate=pl.CostEstimate(
            flops=8 * rows * feats * hidden, bytes_accessed=8 * feats * hidden, transcendentals=rows * hidden
        ),
    )(tokens, out_grad, w_in, b_in, w_out)
    block_out, tokens_part, bias_grad, tok, og, act, hg = outs[:7]
    arrived = []
    for step, piece in enumerate(outs[7:], 1):
        to_peer = [(c, (c + step) % col_count) for c in range(col_count)]
        arrived.append(lax.ppermute(piece, "col", to_peer))
    whole_block = lambda i: (0, 0)
    w_in_grad, w_out_grad, block_out = pl.pallas_call(
        weight_kernel,
        grid=(hidden // TILE,),
        out_shape=[
            jax.ShapeDtypeStruct((feats, hidden), BF16),
            jax.ShapeDtypeStruct((hidden, feats), BF16),
            jax.ShapeDtypeStruct((tile_rows, feats), BF16),
        ],
        in_specs=[
            pl.BlockSpec((rows, feats), whole_block),
            pl.BlockSpec((rows, feats), whole_block),
            pl.BlockSpec((rows, TILE), lambda i: (0, i)),
            pl.BlockSpec((rows, TILE), lambda i: (0, i)),
            pl.BlockSpec((tile_rows, feats), whole_block),
        ],
        out_specs=[
            pl.BlockSpec((feats, TILE), lambda i: (0, i)),
            pl.BlockSpec((TILE, feats), lambda i: (i, 0)),
            pl.BlockSpec((tile_rows, feats), whole_block),
        ],
        scratch_shapes=[pltpu.VMEM((feats, rows), BF16)],
        compiler_params=pltpu.CompilerParams(vmem_limit_bytes=32 * 2**20),
        cost_estimate=pl.CostEstimate(
            flops=4 * rows * feats * hidden, bytes_accessed=4 * feats * hidden, transcendentals=0
        ),
    )(
        tok.reshape(rows, feats), og.reshape(rows, feats), act.reshape(rows, hidden), hg.reshape(rows, hidden),
        block_out,
    )
    tokens_grad = tokens_part
    for piece in arrived:
        tokens_grad = tokens_grad + piece.astype(F32)
    tokens_grad = tokens_grad.astype(BF16)
    return block_out, tokens_grad, w_in_grad, w_out_grad, bias_grad


def by_shape(mesh):
    def run(tokens, out_grad, w_in, b_in, w_out):
        depth_count = mesh.shape["depth"]
        fits = (
            mesh.shape["row"] == 4
            and depth_count == 2
            and mesh.shape["col"] > 1
            and tokens.shape[0] % 32 == 0
            and tokens.shape[1] % TILE == 0
            and w_in.shape[1] % (depth_count * TILE) == 0
        )
        if fits:
            return fused(mesh.shape["col"], tokens, out_grad, w_in, b_in, w_out)
        return local(tokens, out_grad, w_in, b_in, w_out)

    return run


def solution(mesh):
    return jax.shard_map(
        by_shape(mesh),
        mesh=mesh,
        in_specs=(
            P(("col", "depth"), "row"),
            P(("col", "depth"), "row"),
            P("row", "col"),
            P("col"),
            P("col", "row"),
        ),
        out_specs=(
            P(("col", "depth"), "row"),
            P(("col", "depth"), "row"),
            P("row", ("col", "depth")),
            P(("col", "depth"), "row"),
            P("col"),
        ),
        check_vma=False,
    )
```

```python
import functools

import jax
import jax.numpy as jnp
from jax import lax
from jax.experimental import pallas as pl
from jax.experimental.pallas import tpu as pltpu
from jax.sharding import PartitionSpec as P

root_coeff = 0.7978845608028654
cubic_coeff = 0.044715


def gelu_parts(pre_act):
    inner_arg = root_coeff * (pre_act + cubic_coeff * pre_act * pre_act * pre_act)
    tangent = jnp.tanh(inner_arg)
    gelu_value = 0.5 * pre_act * (1.0 + tangent)
    gelu_slope = 0.5 * (1.0 + tangent) + 0.5 * pre_act * (1.0 - tangent * tangent) * root_coeff * (
        1.0 + 3.0 * cubic_coeff * pre_act * pre_act
    )
    return (gelu_value, gelu_slope)


def right_transposed(left_side, right_side):
    return lax.dot_general(
        left_side, right_side, (((1,), (1,)), ((), ())), preferred_element_type=jnp.float32
    )


def left_transposed(left_side, right_side):
    return lax.dot_general(
        left_side, right_side, (((0,), (0,)), ((), ())), preferred_element_type=jnp.float32
    )


def depth_rows(gathered, col_count, depth_index, depth_count):
    tile_rows = gathered.shape[0] // (col_count * depth_count)
    shaped = gathered.reshape(col_count, depth_count, tile_rows, gathered.shape[1])
    picked = lax.dynamic_index_in_dim(shaped, depth_index, 1, keepdims=False)
    return picked.reshape(col_count * tile_rows, gathered.shape[1])


def local(tokens, out_grad, w_in, b_in, w_out):
    col_count = lax.axis_size("col")
    depth_count = lax.axis_size("depth")
    tile_rows = tokens.shape[0]
    part_cols = w_in.shape[1] // depth_count
    depth_index = lax.axis_index("depth")
    all_input, all_grad = (
        lax.all_gather(tokens, ("col", "depth"), axis=0, tiled=True),
        lax.all_gather(out_grad, ("col", "depth"), axis=0, tiled=True),
    )
    plane_input = depth_rows(all_input, col_count, depth_index, depth_count)
    plane_grad = depth_rows(all_grad, col_count, depth_index, depth_count)
    pre_sum = lax.psum_scatter(
        jnp.dot(plane_input, w_in, preferred_element_type=jnp.float32),
        "row",
        scatter_dimension=0,
        tiled=True,
    )
    pre_share = pre_sum + b_in
    gelu_value, gelu_slope = gelu_parts(pre_share)
    plane_act = lax.all_gather(gelu_value.astype(jnp.bfloat16), "row", axis=0, tiled=True)
    block_out = lax.psum_scatter(
        jnp.dot(plane_act, w_out, preferred_element_type=jnp.float32),
        "col",
        scatter_dimension=0,
        tiled=True,
    ).astype(jnp.bfloat16)
    grad_share = lax.psum_scatter(
        right_transposed(plane_grad, w_out), "row", scatter_dimension=0, tiled=True
    )
    pre_grad = grad_share * gelu_slope
    plane_hgrad = lax.all_gather(pre_grad.astype(jnp.bfloat16), "row", axis=0, tiled=True)
    b_in_grad = lax.psum(jnp.sum(pre_grad, axis=0), ("row", "depth"))
    tokens_grad = lax.psum_scatter(
        right_transposed(plane_hgrad, w_in), "col", scatter_dimension=0, tiled=True
    ).astype(jnp.bfloat16)
    act_parts = lax.all_to_all(
        plane_act.reshape(col_count, tile_rows, w_in.shape[1]),
        "depth",
        split_axis=2,
        concat_axis=1,
        tiled=True,
    )
    act_parts = act_parts.reshape(-1, part_cols)
    hgrad_parts = lax.all_to_all(
        plane_hgrad.reshape(col_count, tile_rows, w_in.shape[1]),
        "depth",
        split_axis=2,
        concat_axis=1,
        tiled=True,
    )
    hgrad_parts = hgrad_parts.reshape(-1, part_cols)
    w_in_grad = left_transposed(all_input, hgrad_parts)
    w_out_grad = left_transposed(act_parts, all_grad)
    return (
        block_out,
        tokens_grad,
        w_in_grad.astype(jnp.bfloat16),
        w_out_grad.astype(jnp.bfloat16),
        b_in_grad,
    )


MESH = pl.DeviceIdType.MESH
TILE = 256
BF16 = jnp.bfloat16
F32 = jnp.float32


def block_kernel(
    col_count,
    tokens_ref, grad_ref, w_in_ref, bias_ref, w_out_ref,
    *refs,
):
    away = col_count - 1
    out_ref, tgrad_ref, bgrad_ref, tok_out, og_out, act_out, hg_out = refs[:7]
    tgrad_away = refs[7:7 + away]
    (
    tok, og, w_in, w_out, bias, b_all, part, part16, core_in, chip16, y_in, act, hg, slope,
    x_out, x_in, z_sum, z_out, z_in, b_acc, b_core, b_own, b_x,
    local_sem, z_ssem, z_rsem, x_ssem, x_rsem, c_ssem, c_rsem, y_ssem, y_rsem,
    a_ssem, a_rsem, rx_ssem, rx_rsem, rz_ssem, rz_rsem, b_ssem, b_rsem, out_sem,
    ) = refs[7 + away:]
    row = lax.axis_index("row")
    col = lax.axis_index("col")
    depth = lax.axis_index("depth")
    core = lax.rem(row, 2)
    core_peer = {"row": row + 1 - 2 * core}
    y_peer = {"row": lax.rem(row + 2, 4)}
    x_peer = {"depth": 1 - depth}
    hidden = w_in.shape[1]
    feats = w_in.shape[0]
    half = part.shape[4]

    def z_peer(step):
        return {"col": lax.rem(col + step, col_count)}

    def remote(src, dst, ssem, rsem, peer):
        return pltpu.make_async_remote_copy(
            src_ref=src, dst_ref=dst, send_sem=ssem, recv_sem=rsem, device_id=peer, device_id_type=MESH
        )

    base = pl.multiple_of(depth * hidden, 128)
    locals_ = [
        pltpu.make_async_copy(tokens_ref, tok.at[0, 0], local_sem.at[0]),
        pltpu.make_async_copy(w_in_ref.at[:, pl.ds(base, hidden)], w_in, local_sem.at[1]),
        pltpu.make_async_copy(grad_ref, og.at[0, 0], local_sem.at[2]),
        pltpu.make_async_copy(w_out_ref.at[pl.ds(base, hidden), :], w_out, local_sem.at[3]),
        pltpu.make_async_copy(bias_ref, bias, local_sem.at[4]),
    ]
    for copy in locals_:
        copy.start()

    barrier = pltpu.get_barrier_semaphore()
    peers = [z_peer(step) for step in range(1, col_count)] + [x_peer, y_peer, core_peer]
    for peer in peers:
        pl.semaphore_signal(barrier, inc=1, device_id=peer, device_id_type=MESH)
    pl.semaphore_wait(barrier, len(peers))

    sends = []

    def start(copy):
        copy.start()
        sends.append(copy)
        return copy

    def pair_start(which, src, dst):
        start(remote(src, dst.at[1, 0], x_ssem.at[which, 0], x_rsem.at[which, 0], x_peer))

    def line_start(which, src, dst):
        for step in range(1, col_count):
            start(remote(src, dst.at[0, step], z_ssem.at[which, step], z_rsem.at[which, step], z_peer(step)))

    def gather_own(which, dst):
        for step in range(1, col_count):
            block = dst.at[0, step]
            remote(block, block, z_ssem.at[which, step], z_rsem.at[which, step], z_peer(step)).wait_recv()
            start(remote(block, dst.at[1, step], x_ssem.at[which, step], x_rsem.at[which, step], x_peer))

    def other_wait(which, dst, step):
        block = dst.at[1, step]
        remote(block, block, x_ssem.at[which, step], x_rsem.at[which, step], x_peer).wait_recv()

    def gather_other(which, dst):
        for step in range(1, col_count):
            other_wait(which, dst, step)

    def tile_of(i):
        return pl.ds(pl.multiple_of(i * TILE, TILE), TILE)

    def cut(group):
        return pl.ds(group[1][0], len(group[1])), pl.ds(group[2][0], len(group[2]))

    def rows_of(buf, group):
        value = buf[(*cut(group),)]
        return value.reshape(-1, value.shape[-1])

    def places(group):
        return [(chunk, s) for chunk in group[1] for s in group[2]]

    def product(which, group, multiply):
        @pl.loop(0, hidden // TILE)
        def _(i):
            at = tile_of(i)
            value = multiply(rows_of(og if which else tok, group), at)
            for n, (chunk, s) in enumerate(places(group)):
                for k in range(2):
                    piece = value[(2 * n + k) * half:(2 * n + k + 1) * half]
                    part[which, k, chunk, s, :, at] = piece
                    part16[which, k, chunk, s, :, at] = piece.astype(BF16)

        start(remote(
            part16.at[(which, 1 - core, *cut(group))], core_in.at[(which, *cut(group))],
            c_ssem.at[which, group[0]], c_rsem.at[which, group[0]], core_peer,
        ))

    def chip_sum(which, group):
        landed = core_in.at[(which, *cut(group))]
        remote(landed, landed, c_ssem.at[which, group[0]], c_rsem.at[which, group[0]], core_peer).wait_recv()

        @pl.loop(0, hidden // TILE)
        def _(i):
            at = tile_of(i)
            for chunk, s in places(group):
                total = part[which, core, chunk, s, :, at] + core_in[which, chunk, s, :, at].astype(F32)
                chip16[which, chunk, s, :, at] = total.astype(BF16)

        start(remote(
            chip16.at[(which, *cut(group))], y_in.at[(which, *cut(group))],
            y_ssem.at[which, group[0]], y_rsem.at[which, group[0]], y_peer,
        ))

    def y_wait(which, group):
        landed = y_in.at[(which, *cut(group))]
        remote(landed, landed, y_ssem.at[which, group[0]], y_rsem.at[which, group[0]], y_peer).wait_recv()

    def row_sum(which, chunk, s, at):
        return chip16[which, chunk, s, :, at].astype(F32) + y_in[which, chunk, s, :, at].astype(F32)

    def share(which, group, buf, whose):
        piece = buf.at[(*cut(group), whose)]
        return remote(piece, piece, a_ssem.at[which, group[0]], a_rsem.at[which, group[0]], core_peer)

    def activate(group):
        y_wait(0, group)

        @pl.loop(0, hidden // TILE)
        def _(i):
            at = tile_of(i)
            bias_here = b_all[:, pl.ds(pl.multiple_of(depth * hidden + i * TILE, 128), TILE)]
            for chunk, s in places(group):
                value, slope_here = gelu_parts(row_sum(0, chunk, s, at) + bias_here)
                act[chunk, s, core, :, at] = value.astype(BF16)
                slope[chunk, s, :, at] = slope_here

        start(share(0, group, act, core))

    def hidden_grad(group, fresh):
        y_wait(1, group)

        @pl.loop(0, hidden // TILE)
        def _(i):
            at = tile_of(i)
            total = None if fresh else b_acc[:, at]
            for chunk, s in places(group):
                pre_grad = row_sum(1, chunk, s, at) * slope[chunk, s, :, at]
                hg[chunk, s, core, :, at] = pre_grad.astype(BF16)
                here = jnp.sum(pre_grad, axis=0, keepdims=True)
                total = here if total is None else total + here
            b_acc[:, at] = total

        start(share(1, group, hg, core))

    def project(which, chunk, buf, multiply):
        tile_rows = x_out.shape[2]

        @pl.loop(0, feats // TILE)
        def _(i):
            at = tile_of(i)
            value = multiply(rows_of(buf, (0, (chunk,), range(col_count))), at)
            for c in range(col_count):
                piece = value[c * tile_rows:(c + 1) * tile_rows]
                if chunk == 1:
                    x_out[which, c, :, at] = piece.astype(BF16)
                else:
                    z_sum[which, c, :, at] = piece

        if chunk == 1:
            start(remote(x_out.at[which], x_in.at[which], rx_ssem.at[which], rx_rsem.at[which], x_peer))

    def plane_sum(which):
        landed = x_in.at[which]
        remote(landed, landed, rx_ssem.at[which], rx_rsem.at[which], x_peer).wait_recv()
        for c in range(col_count):
            total = z_sum[which, c] + x_in[which, c].astype(F32)
            z_sum[which, c] = total
            z_out[which, c] = total.astype(BF16)
        for step in range(1, col_count):
            start(remote(
                z_out.at[which, col_count - step], z_in.at[which, step - 1],
                rz_ssem.at[which, step - 1], rz_rsem.at[which, step - 1], z_peer(step),
            ))

    def final_sum(which, result):
        for step in range(1, col_count):
            landed = z_in.at[which, step - 1]
            remote(
                landed, landed, rz_ssem.at[which, step - 1], rz_rsem.at[which, step - 1], z_peer(step)
            ).wait_recv()
        total = z_sum[which, 0]
        for step in range(1, col_count):
            total = total + z_in[which, step - 1].astype(F32)
        result[...] = total.astype(BF16)

    def keep(which, src, dst):
        copy = pltpu.make_async_copy(src, dst, out_sem.at[which])
        copy.start()
        return copy

    def pre_tile(value, at):
        return jnp.dot(value, w_in[:, at], preferred_element_type=F32)

    def back_tile(value, at):
        return right_transposed(value, w_out[at, :])

    steps = range(1, col_count)
    pair, far, near = (0, (0, 1), (0,)), (1, (1,), steps), (2, (0,), steps)

    pair_start(0, tokens_ref, tok)
    line_start(0, tokens_ref, tok)
    pair_start(1, grad_ref, og)
    locals_[4].wait()
    b_all[...] = bias[...].reshape(1, 2 * hidden)
    locals_[0].wait()
    locals_[1].wait()
    other_wait(0, tok, 0)
    product(0, pair, pre_tile)
    locals_[2].wait()
    locals_[3].wait()
    other_wait(1, og, 0)
    product(1, pair, back_tile)
    chip_sum(0, pair)
    chip_sum(1, pair)
    gather_own(0, tok)
    line_start(1, grad_ref, og)
    product(0, near, pre_tile)
    gather_other(0, tok)
    product(0, far, pre_tile)
    kept = [keep(0, tok, tok_out)]
    chip_sum(0, far)
    chip_sum(0, near)
    gather_own(1, og)
    product(1, near, back_tile)
    activate(pair)
    gather_other(1, og)
    kept.append(keep(1, og, og_out))
    product(1, far, back_tile)
    activate(far)
    chip_sum(1, far)
    chip_sum(1, near)
    share(0, pair, act, 1 - core).wait_recv()
    share(0, far, act, 1 - core).wait_recv()

    def forward(value, at):
        return jnp.dot(value, w_out[:, at], preferred_element_type=F32)

    def backward(value, at):
        return right_transposed(value, w_in[at, :])

    project(0, 1, act, forward)
    activate(near)
    hidden_grad(pair, True)
    share(0, near, act, 1 - core).wait_recv()
    kept.append(keep(2, act, act_out))
    project(0, 0, act, forward)
    hidden_grad(far, False)
    share(1, pair, hg, 1 - core).wait_recv()
    share(1, far, hg, 1 - core).wait_recv()
    project(1, 1, hg, backward)
    plane_sum(0)
    hidden_grad(near, False)
    start(remote(b_acc, b_core, b_ssem.at[0], b_rsem.at[0], core_peer))
    share(1, near, hg, 1 - core).wait_recv()
    kept.append(keep(3, hg, hg_out))
    remote(b_core, b_core, b_ssem.at[0], b_rsem.at[0], core_peer).wait_recv()
    b_own[...] = b_acc[...] + b_core[...]
    start(remote(b_own, b_x, b_ssem.at[1], b_rsem.at[1], x_peer))
    project(1, 0, hg, backward)
    final_sum(0, out_ref)
    landed = x_in.at[1]
    remote(landed, landed, rx_ssem.at[1], rx_rsem.at[1], x_peer).wait_recv()
    tgrad_ref[...] = z_sum[1, 0] + x_in[1, 0].astype(F32)
    for step in range(1, col_count):
        total = z_sum[1, col_count - step] + x_in[1, col_count - step].astype(F32)
        tgrad_away[step - 1][...] = total.astype(BF16)
    remote(b_x, b_x, b_ssem.at[1], b_rsem.at[1], x_peer).wait_recv()
    b_all[:, pl.ds(base, hidden)] = b_own[...]
    b_all[:, pl.ds(pl.multiple_of((1 - depth) * hidden, 128), hidden)] = b_x[...]
    bgrad_ref[...] = b_all[...].reshape(2 * hidden)
    for copy in kept:
        copy.wait()
    for copy in sends:
        copy.wait_send()


def weight_kernel(
    tok_ref, og_ref, act_ref, hg_ref, out_ref, w_in_grad_ref, w_out_grad_ref, out_again, tok_turned,
):
    @pl.when(pl.program_id(0) == 0)
    def _():
        tok_turned[...] = tok_ref[...].T
        out_again[...] = out_ref[...]

    w_in_grad_ref[...] = jnp.dot(tok_turned[...], hg_ref[...], preferred_element_type=F32).astype(BF16)
    w_out_grad_ref[...] = left_transposed(act_ref[...], og_ref[...]).astype(BF16)


def fused(col_count, tokens, out_grad, w_in, b_in, w_out):
    tile_rows, feats = tokens.shape
    hidden = w_in.shape[1] // 2
    plane = col_count * tile_rows
    half = tile_rows // 2
    rows = 2 * plane
    anywhere = pl.BlockSpec(memory_space=pltpu.HBM)
    vmem = pl.BlockSpec(memory_space=pltpu.VMEM)
    dma = pltpu.SemaphoreType.DMA
    outs = pl.pallas_call(
        functools.partial(block_kernel, col_count),
        out_shape=[
            jax.ShapeDtypeStruct((tile_rows, feats), BF16),
            jax.ShapeDtypeStruct((tile_rows, feats), F32),
            jax.ShapeDtypeStruct((2 * hidden,), F32),
            jax.ShapeDtypeStruct((2, col_count, tile_rows, feats), BF16),
            jax.ShapeDtypeStruct((2, col_count, tile_rows, feats), BF16),
            jax.ShapeDtypeStruct((2, col_count, 2, half, hidden), BF16),
            jax.ShapeDtypeStruct((2, col_count, 2, half, hidden), BF16),
        ] + [jax.ShapeDtypeStruct((tile_rows, feats), BF16)] * (col_count - 1),
        in_specs=[anywhere] * 5,
        out_specs=[vmem, vmem, vmem, anywhere, anywhere, anywhere, anywhere] + [vmem] * (col_count - 1),
        scratch_shapes=[
            pltpu.VMEM((2, col_count, tile_rows, feats), BF16),
            pltpu.VMEM((2, col_count, tile_rows, feats), BF16),
            pltpu.VMEM((feats, hidden), BF16),
            pltpu.VMEM((hidden, feats), BF16),
            pltpu.VMEM((2 * hidden,), F32),
            pltpu.VMEM((1, 2 * hidden), F32),
            pltpu.VMEM((2, 2, 2, col_count, half, hidden), F32),
            pltpu.VMEM((2, 2, 2, col_count, half, hidden), BF16),
            pltpu.VMEM((2, 2, col_count, half, hidden), BF16),
            pltpu.VMEM((2, 2, col_count, half, hidden), BF16),
            pltpu.VMEM((2, 2, col_count, half, hidden), BF16),
            pltpu.VMEM((2, col_count, 2, half, hidden), BF16),
            pltpu.VMEM((2, col_count, 2, half, hidden), BF16),
            pltpu.VMEM((2, col_count, half, hidden), F32),
            pltpu.VMEM((2, col_count, tile_rows, feats), BF16),
            pltpu.VMEM((2, col_count, tile_rows, feats), BF16),
            pltpu.VMEM((2, col_count, tile_rows, feats), F32),
            pltpu.VMEM((2, col_count, tile_rows, feats), BF16),
            pltpu.VMEM((2, col_count - 1, tile_rows, feats), BF16),
            pltpu.VMEM((1, hidden), F32),
            pltpu.VMEM((1, hidden), F32),
            pltpu.VMEM((1, hidden), F32),
            pltpu.VMEM((1, hidden), F32),
            dma((5,)),
            dma((2, col_count)),
            dma((2, col_count)),
            dma((2, col_count)),
            dma((2, col_count)),
            dma((2, 3)),
            dma((2, 3)),
            dma((2, 3)),
            dma((2, 3)),
            dma((2, 3)),
            dma((2, 3)),
            dma((2,)),
            dma((2,)),
            dma((2, col_count - 1)),
            dma((2, col_count - 1)),
            dma((2,)),
            dma((2,)),
            dma((4,)),
        ],
        compiler_params=pltpu.CompilerParams(
            collective_id=0, has_side_effects=True, vmem_limit_bytes=44 * 2**20
        ),
        cost_estimate=pl.CostEstimate(
            flops=8 * rows * feats * hidden, bytes_accessed=8 * feats * hidden, transcendentals=rows * hidden
        ),
    )(tokens, out_grad, w_in, b_in, w_out)
    block_out, tokens_part, bias_grad, tok, og, act, hg = outs[:7]
    arrived = []
    for step, piece in enumerate(outs[7:], 1):
        to_peer = [(c, (c + step) % col_count) for c in range(col_count)]
        arrived.append(lax.ppermute(piece, "col", to_peer))
    whole_block = lambda i: (0, 0)
    w_in_grad, w_out_grad, block_out = pl.pallas_call(
        weight_kernel,
        grid=(hidden // TILE,),
        out_shape=[
            jax.ShapeDtypeStruct((feats, hidden), BF16),
            jax.ShapeDtypeStruct((hidden, feats), BF16),
            jax.ShapeDtypeStruct((tile_rows, feats), BF16),
        ],
        in_specs=[
            pl.BlockSpec((rows, feats), whole_block),
            pl.BlockSpec((rows, feats), whole_block),
            pl.BlockSpec((rows, TILE), lambda i: (0, i)),
            pl.BlockSpec((rows, TILE), lambda i: (0, i)),
            pl.BlockSpec((tile_rows, feats), whole_block),
        ],
        out_specs=[
            pl.BlockSpec((feats, TILE), lambda i: (0, i)),
            pl.BlockSpec((TILE, feats), lambda i: (i, 0)),
            pl.BlockSpec((tile_rows, feats), whole_block),
        ],
        scratch_shapes=[pltpu.VMEM((feats, rows), BF16)],
        compiler_params=pltpu.CompilerParams(vmem_limit_bytes=32 * 2**20),
        cost_estimate=pl.CostEstimate(
            flops=4 * rows * feats * hidden, bytes_accessed=4 * feats * hidden, transcendentals=0
        ),
    )(
        tok.reshape(rows, feats), og.reshape(rows, feats), act.reshape(rows, hidden), hg.reshape(rows, hidden),
        block_out,
    )
    tokens_grad = tokens_part
    for piece in arrived:
        tokens_grad = tokens_grad + piece.astype(F32)
    tokens_grad = tokens_grad.astype(BF16)
    return block_out, tokens_grad, w_in_grad, w_out_grad, bias_grad


def by_shape(mesh):
    def run(tokens, out_grad, w_in, b_in, w_out):
        depth_count = mesh.shape["depth"]
        fits = (
            mesh.shape["row"] == 4
            and depth_count == 2
            and mesh.shape["col"] > 1
            and tokens.shape[0] % 32 == 0
            and tokens.shape[1] % TILE == 0
            and w_in.shape[1] % (depth_count * TILE) == 0
        )
        if fits:
            return fused(mesh.shape["col"], tokens, out_grad, w_in, b_in, w_out)
        return local(tokens, out_grad, w_in, b_in, w_out)

    return run


def solution(mesh):
    return jax.shard_map(
        by_shape(mesh),
        mesh=mesh,
        in_specs=(
            P(("col", "depth"), "row"),
            P(("col", "depth"), "row"),
            P("row", "col"),
            P("col"),
            P("col", "row"),
        ),
        out_specs=(
            P(("col", "depth"), "row"),
            P(("col", "depth"), "row"),
            P("row", ("col", "depth")),
            P(("col", "depth"), "row"),
            P("col"),
        ),
        check_vma=False,
    )
```

```python
import functools

import jax
import jax.numpy as jnp
from jax import lax
from jax.experimental import pallas as pl
from jax.experimental.pallas import tpu as pltpu
from jax.sharding import PartitionSpec as P

root_coeff = 0.7978845608028654
cubic_coeff = 0.044715


def gelu_parts(pre_act):
    inner_arg = root_coeff * (pre_act + cubic_coeff * pre_act * pre_act * pre_act)
    tangent = jnp.tanh(inner_arg)
    gelu_value = 0.5 * pre_act * (1.0 + tangent)
    gelu_slope = 0.5 * (1.0 + tangent) + 0.5 * pre_act * (1.0 - tangent * tangent) * root_coeff * (
        1.0 + 3.0 * cubic_coeff * pre_act * pre_act
    )
    return (gelu_value, gelu_slope)


def right_transposed(left_side, right_side):
    return lax.dot_general(
        left_side, right_side, (((1,), (1,)), ((), ())), preferred_element_type=jnp.float32
    )


def left_transposed(left_side, right_side):
    return lax.dot_general(
        left_side, right_side, (((0,), (0,)), ((), ())), preferred_element_type=jnp.float32
    )


def depth_rows(gathered, col_count, depth_index, depth_count):
    tile_rows = gathered.shape[0] // (col_count * depth_count)
    shaped = gathered.reshape(col_count, depth_count, tile_rows, gathered.shape[1])
    picked = lax.dynamic_index_in_dim(shaped, depth_index, 1, keepdims=False)
    return picked.reshape(col_count * tile_rows, gathered.shape[1])


def local(tokens, out_grad, w_in, b_in, w_out):
    col_count = lax.axis_size("col")
    depth_count = lax.axis_size("depth")
    tile_rows = tokens.shape[0]
    part_cols = w_in.shape[1] // depth_count
    depth_index = lax.axis_index("depth")
    all_input, all_grad = (
        lax.all_gather(tokens, ("col", "depth"), axis=0, tiled=True),
        lax.all_gather(out_grad, ("col", "depth"), axis=0, tiled=True),
    )
    plane_input = depth_rows(all_input, col_count, depth_index, depth_count)
    plane_grad = depth_rows(all_grad, col_count, depth_index, depth_count)
    pre_sum = lax.psum_scatter(
        jnp.dot(plane_input, w_in, preferred_element_type=jnp.float32),
        "row",
        scatter_dimension=0,
        tiled=True,
    )
    pre_share = pre_sum + b_in
    gelu_value, gelu_slope = gelu_parts(pre_share)
    plane_act = lax.all_gather(gelu_value.astype(jnp.bfloat16), "row", axis=0, tiled=True)
    block_out = lax.psum_scatter(
        jnp.dot(plane_act, w_out, preferred_element_type=jnp.float32),
        "col",
        scatter_dimension=0,
        tiled=True,
    ).astype(jnp.bfloat16)
    grad_share = lax.psum_scatter(
        right_transposed(plane_grad, w_out), "row", scatter_dimension=0, tiled=True
    )
    pre_grad = grad_share * gelu_slope
    plane_hgrad = lax.all_gather(pre_grad.astype(jnp.bfloat16), "row", axis=0, tiled=True)
    b_in_grad = lax.psum(jnp.sum(pre_grad, axis=0), ("row", "depth"))
    tokens_grad = lax.psum_scatter(
        right_transposed(plane_hgrad, w_in), "col", scatter_dimension=0, tiled=True
    ).astype(jnp.bfloat16)
    act_parts = lax.all_to_all(
        plane_act.reshape(col_count, tile_rows, w_in.shape[1]),
        "depth",
        split_axis=2,
        concat_axis=1,
        tiled=True,
    )
    act_parts = act_parts.reshape(-1, part_cols)
    hgrad_parts = lax.all_to_all(
        plane_hgrad.reshape(col_count, tile_rows, w_in.shape[1]),
        "depth",
        split_axis=2,
        concat_axis=1,
        tiled=True,
    )
    hgrad_parts = hgrad_parts.reshape(-1, part_cols)
    w_in_grad = left_transposed(all_input, hgrad_parts)
    w_out_grad = left_transposed(act_parts, all_grad)
    return (
        block_out,
        tokens_grad,
        w_in_grad.astype(jnp.bfloat16),
        w_out_grad.astype(jnp.bfloat16),
        b_in_grad,
    )


MESH = pl.DeviceIdType.MESH
TILE = 256
BF16 = jnp.bfloat16
F32 = jnp.float32


def block_kernel(
    col_count,
    tokens_ref, grad_ref, w_in_ref, bias_ref, w_out_ref,
    *refs,
):
    away = col_count - 1
    out_ref, tgrad_ref, bgrad_ref, tok_out, og_out, act_out, hg_out = refs[:7]
    tgrad_away = refs[7:7 + away]
    (
    tok, og, w_in, w_out, bias, b_all, part, part16, core_in, chip16, y_in, act, hg, slope,
    x_out, x_in, z_sum, z_out, z_in, b_acc, b_core, b_own, b_x,
    local_sem, z_ssem, z_rsem, x_ssem, x_rsem, c_ssem, c_rsem, y_ssem, y_rsem,
    a_ssem, a_rsem, rx_ssem, rx_rsem, rz_ssem, rz_rsem, b_ssem, b_rsem, out_sem,
    ) = refs[7 + away:]
    row = lax.axis_index("row")
    col = lax.axis_index("col")
    depth = lax.axis_index("depth")
    core = lax.rem(row, 2)
    core_peer = {"row": row + 1 - 2 * core}
    y_peer = {"row": lax.rem(row + 2, 4)}
    x_peer = {"depth": 1 - depth}
    hidden = w_in.shape[1]
    feats = w_in.shape[0]
    half = part.shape[4]

    def z_peer(step):
        return {"col": lax.rem(col + step, col_count)}

    def remote(src, dst, ssem, rsem, peer):
        return pltpu.make_async_remote_copy(
            src_ref=src, dst_ref=dst, send_sem=ssem, recv_sem=rsem, device_id=peer, device_id_type=MESH
        )

    base = pl.multiple_of(depth * hidden, 128)
    locals_ = [
        pltpu.make_async_copy(tokens_ref, tok.at[0, 0], local_sem.at[0]),
        pltpu.make_async_copy(w_in_ref.at[:, pl.ds(base, hidden)], w_in, local_sem.at[1]),
        pltpu.make_async_copy(grad_ref, og.at[0, 0], local_sem.at[2]),
        pltpu.make_async_copy(w_out_ref.at[pl.ds(base, hidden), :], w_out, local_sem.at[3]),
        pltpu.make_async_copy(bias_ref, bias, local_sem.at[4]),
    ]
    for copy in locals_:
        copy.start()

    barrier = pltpu.get_barrier_semaphore()
    peers = [z_peer(step) for step in range(1, col_count)] + [x_peer, y_peer, core_peer]
    for peer in peers:
        pl.semaphore_signal(barrier, inc=1, device_id=peer, device_id_type=MESH)
    pl.semaphore_wait(barrier, len(peers))

    sends = []

    def start(copy):
        copy.start()
        sends.append(copy)
        return copy

    def pair_start(which, src, dst):
        start(remote(src, dst.at[1, 0], x_ssem.at[which, 0], x_rsem.at[which, 0], x_peer))

    def line_start(which, src, dst):
        for step in range(1, col_count):
            start(remote(src, dst.at[0, step], z_ssem.at[which, step], z_rsem.at[which, step], z_peer(step)))

    def gather_own(which, dst):
        for step in range(1, col_count):
            block = dst.at[0, step]
            remote(block, block, z_ssem.at[which, step], z_rsem.at[which, step], z_peer(step)).wait_recv()
            start(remote(block, dst.at[1, step], x_ssem.at[which, step], x_rsem.at[which, step], x_peer))

    def other_wait(which, dst, step):
        block = dst.at[1, step]
        remote(block, block, x_ssem.at[which, step], x_rsem.at[which, step], x_peer).wait_recv()

    def gather_other(which, dst):
        for step in range(1, col_count):
            other_wait(which, dst, step)

    def tile_of(i):
        return pl.ds(pl.multiple_of(i * TILE, TILE), TILE)

    def cut(group):
        return pl.ds(group[1][0], len(group[1])), pl.ds(group[2][0], len(group[2]))

    def rows_of(buf, group):
        value = buf[(*cut(group),)]
        return value.reshape(-1, value.shape[-1])

    def places(group):
        return [(chunk, s) for chunk in group[1] for s in group[2]]

    def product(which, group, multiply, parts):
        @pl.loop(0, hidden // TILE, unroll=True)
        def _(i):
            at = tile_of(i)
            value = multiply(rows_of(og if which else tok, group), at)
            for n, (chunk, s) in enumerate(places(group)):
                for k in range(2):
                    piece = value[(2 * n + k) * half:(2 * n + k + 1) * half]
                    part[which, k, chunk, s, :, at] = piece
                    part16[which, k, chunk, s, :, at] = piece.astype(BF16)

        for group in parts:
            start(remote(
                part16.at[(which, 1 - core, *cut(group))], core_in.at[(which, *cut(group))],
                c_ssem.at[which, group[0]], c_rsem.at[which, group[0]], core_peer,
            ))

    def chip_sum(which, group):
        landed = core_in.at[(which, *cut(group))]
        remote(landed, landed, c_ssem.at[which, group[0]], c_rsem.at[which, group[0]], core_peer).wait_recv()

        @pl.loop(0, hidden // TILE)
        def _(i):
            at = tile_of(i)
            for chunk, s in places(group):
                total = part[which, core, chunk, s, :, at] + core_in[which, chunk, s, :, at].astype(F32)
                chip16[which, chunk, s, :, at] = total.astype(BF16)

        start(remote(
            chip16.at[(which, *cut(group))], y_in.at[(which, *cut(group))],
            y_ssem.at[which, group[0]], y_rsem.at[which, group[0]], y_peer,
        ))

    def y_wait(which, group):
        landed = y_in.at[(which, *cut(group))]
        remote(landed, landed, y_ssem.at[which, group[0]], y_rsem.at[which, group[0]], y_peer).wait_recv()

    def row_sum(which, chunk, s, at):
        return chip16[which, chunk, s, :, at].astype(F32) + y_in[which, chunk, s, :, at].astype(F32)

    def share(which, group, buf, whose):
        piece = buf.at[(*cut(group), whose)]
        return remote(piece, piece, a_ssem.at[which, group[0]], a_rsem.at[which, group[0]], core_peer)

    def activate(group):
        y_wait(0, group)

        @pl.loop(0, hidden // TILE)
        def _(i):
            at = tile_of(i)
            bias_here = b_all[:, pl.ds(pl.multiple_of(depth * hidden + i * TILE, 128), TILE)]
            for chunk, s in places(group):
                value, slope_here = gelu_parts(row_sum(0, chunk, s, at) + bias_here)
                act[chunk, s, core, :, at] = value.astype(BF16)
                slope[chunk, s, :, at] = slope_here

        start(share(0, group, act, core))

    def hidden_grad(group, fresh):
        y_wait(1, group)

        @pl.loop(0, hidden // TILE)
        def _(i):
            at = tile_of(i)
            total = None if fresh else b_acc[:, at]
            for chunk, s in places(group):
                pre_grad = row_sum(1, chunk, s, at) * slope[chunk, s, :, at]
                hg[chunk, s, core, :, at] = pre_grad.astype(BF16)
                here = jnp.sum(pre_grad, axis=0, keepdims=True)
                total = here if total is None else total + here
            b_acc[:, at] = total

        start(share(1, group, hg, core))

    def project(which, chunk, buf, multiply):
        tile_rows = x_out.shape[2]

        @pl.loop(0, feats // TILE, unroll=True)
        def _(i):
            at = tile_of(i)
            value = multiply(rows_of(buf, (0, (chunk,), range(col_count))), at)
            for c in range(col_count):
                piece = value[c * tile_rows:(c + 1) * tile_rows]
                if chunk == 1:
                    x_out[which, c, :, at] = piece.astype(BF16)
                else:
                    z_sum[which, c, :, at] = piece

        if chunk == 1:
            start(remote(x_out.at[which], x_in.at[which], rx_ssem.at[which], rx_rsem.at[which], x_peer))

    def plane_sum(which):
        landed = x_in.at[which]
        remote(landed, landed, rx_ssem.at[which], rx_rsem.at[which], x_peer).wait_recv()
        for c in range(col_count):
            total = z_sum[which, c] + x_in[which, c].astype(F32)
            z_sum[which, c] = total
            z_out[which, c] = total.astype(BF16)
        for step in range(1, col_count):
            start(remote(
                z_out.at[which, col_count - step], z_in.at[which, step - 1],
                rz_ssem.at[which, step - 1], rz_rsem.at[which, step - 1], z_peer(step),
            ))

    def final_sum(which, result):
        for step in range(1, col_count):
            landed = z_in.at[which, step - 1]
            remote(
                landed, landed, rz_ssem.at[which, step - 1], rz_rsem.at[which, step - 1], z_peer(step)
            ).wait_recv()
        total = z_sum[which, 0]
        for step in range(1, col_count):
            total = total + z_in[which, step - 1].astype(F32)
        result[...] = total.astype(BF16)

    def keep(which, src, dst):
        copy = pltpu.make_async_copy(src, dst, out_sem.at[which])
        copy.start()
        return copy

    def pre_tile(value, at):
        return jnp.dot(value, w_in[:, at], preferred_element_type=F32)

    def back_tile(value, at):
        return right_transposed(value, w_out[at, :])

    steps = range(1, col_count)
    pair, far, near = (0, (0, 1), (0,)), (1, (1,), steps), (2, (0,), steps)
    rest = (None, (0, 1), steps)

    pair_start(0, tokens_ref, tok)
    line_start(0, tokens_ref, tok)
    pair_start(1, grad_ref, og)
    locals_[4].wait()
    b_all[...] = bias[...].reshape(1, 2 * hidden)
    locals_[0].wait()
    locals_[1].wait()
    other_wait(0, tok, 0)
    product(0, pair, pre_tile, [pair])
    locals_[2].wait()
    locals_[3].wait()
    other_wait(1, og, 0)
    product(1, pair, back_tile, [pair])
    chip_sum(0, pair)
    chip_sum(1, pair)
    gather_own(0, tok)
    line_start(1, grad_ref, og)
    gather_other(0, tok)
    product(0, rest, pre_tile, [far, near])
    kept = [keep(0, tok, tok_out)]
    chip_sum(0, far)
    chip_sum(0, near)
    gather_own(1, og)
    activate(pair)
    gather_other(1, og)
    kept.append(keep(1, og, og_out))
    product(1, rest, back_tile, [far, near])
    activate(far)
    chip_sum(1, far)
    chip_sum(1, near)
    share(0, pair, act, 1 - core).wait_recv()
    share(0, far, act, 1 - core).wait_recv()

    def forward(value, at):
        return jnp.dot(value, w_out[:, at], preferred_element_type=F32)

    def backward(value, at):
        return right_transposed(value, w_in[at, :])

    project(0, 1, act, forward)
    activate(near)
    hidden_grad(pair, True)
    share(0, near, act, 1 - core).wait_recv()
    kept.append(keep(2, act, act_out))
    project(0, 0, act, forward)
    hidden_grad(far, False)
    share(1, pair, hg, 1 - core).wait_recv()
    share(1, far, hg, 1 - core).wait_recv()
    project(1, 1, hg, backward)
    plane_sum(0)
    hidden_grad(near, False)
    start(remote(b_acc, b_core, b_ssem.at[0], b_rsem.at[0], core_peer))
    share(1, near, hg, 1 - core).wait_recv()
    kept.append(keep(3, hg, hg_out))
    remote(b_core, b_core, b_ssem.at[0], b_rsem.at[0], core_peer).wait_recv()
    b_own[...] = b_acc[...] + b_core[...]
    start(remote(b_own, b_x, b_ssem.at[1], b_rsem.at[1], x_peer))
    project(1, 0, hg, backward)
    final_sum(0, out_ref)
    landed = x_in.at[1]
    remote(landed, landed, rx_ssem.at[1], rx_rsem.at[1], x_peer).wait_recv()
    tgrad_ref[...] = z_sum[1, 0] + x_in[1, 0].astype(F32)
    for step in range(1, col_count):
        total = z_sum[1, col_count - step] + x_in[1, col_count - step].astype(F32)
        tgrad_away[step - 1][...] = total.astype(BF16)
    remote(b_x, b_x, b_ssem.at[1], b_rsem.at[1], x_peer).wait_recv()
    b_all[:, pl.ds(base, hidden)] = b_own[...]
    b_all[:, pl.ds(pl.multiple_of((1 - depth) * hidden, 128), hidden)] = b_x[...]
    bgrad_ref[...] = b_all[...].reshape(2 * hidden)
    for copy in kept:
        copy.wait()
    for copy in sends:
        copy.wait_send()


def weight_kernel(
    tok_ref, og_ref, act_ref, hg_ref, out_ref, w_in_grad_ref, w_out_grad_ref, out_again, tok_turned,
):
    @pl.when(pl.program_id(0) == 0)
    def _():
        tok_turned[...] = tok_ref[...].T
        out_again[...] = out_ref[...]

    w_in_grad_ref[...] = jnp.dot(tok_turned[...], hg_ref[...], preferred_element_type=F32).astype(BF16)
    w_out_grad_ref[...] = left_transposed(act_ref[...], og_ref[...]).astype(BF16)


def fused(col_count, tokens, out_grad, w_in, b_in, w_out):
    tile_rows, feats = tokens.shape
    hidden = w_in.shape[1] // 2
    plane = col_count * tile_rows
    half = tile_rows // 2
    rows = 2 * plane
    anywhere = pl.BlockSpec(memory_space=pltpu.HBM)
    vmem = pl.BlockSpec(memory_space=pltpu.VMEM)
    dma = pltpu.SemaphoreType.DMA
    outs = pl.pallas_call(
        functools.partial(block_kernel, col_count),
        out_shape=[
            jax.ShapeDtypeStruct((tile_rows, feats), BF16),
            jax.ShapeDtypeStruct((tile_rows, feats), F32),
            jax.ShapeDtypeStruct((2 * hidden,), F32),
            jax.ShapeDtypeStruct((2, col_count, tile_rows, feats), BF16),
            jax.ShapeDtypeStruct((2, col_count, tile_rows, feats), BF16),
            jax.ShapeDtypeStruct((2, col_count, 2, half, hidden), BF16),
            jax.ShapeDtypeStruct((2, col_count, 2, half, hidden), BF16),
        ] + [jax.ShapeDtypeStruct((tile_rows, feats), BF16)] * (col_count - 1),
        in_specs=[anywhere] * 5,
        out_specs=[vmem, vmem, vmem, anywhere, anywhere, anywhere, anywhere] + [vmem] * (col_count - 1),
        scratch_shapes=[
            pltpu.VMEM((2, col_count, tile_rows, feats), BF16),
            pltpu.VMEM((2, col_count, tile_rows, feats), BF16),
            pltpu.VMEM((feats, hidden), BF16),
            pltpu.VMEM((hidden, feats), BF16),
            pltpu.VMEM((2 * hidden,), F32),
            pltpu.VMEM((1, 2 * hidden), F32),
            pltpu.VMEM((2, 2, 2, col_count, half, hidden), F32),
            pltpu.VMEM((2, 2, 2, col_count, half, hidden), BF16),
            pltpu.VMEM((2, 2, col_count, half, hidden), BF16),
            pltpu.VMEM((2, 2, col_count, half, hidden), BF16),
            pltpu.VMEM((2, 2, col_count, half, hidden), BF16),
            pltpu.VMEM((2, col_count, 2, half, hidden), BF16),
            pltpu.VMEM((2, col_count, 2, half, hidden), BF16),
            pltpu.VMEM((2, col_count, half, hidden), F32),
            pltpu.VMEM((2, col_count, tile_rows, feats), BF16),
            pltpu.VMEM((2, col_count, tile_rows, feats), BF16),
            pltpu.VMEM((2, col_count, tile_rows, feats), F32),
            pltpu.VMEM((2, col_count, tile_rows, feats), BF16),
            pltpu.VMEM((2, col_count - 1, tile_rows, feats), BF16),
            pltpu.VMEM((1, hidden), F32),
            pltpu.VMEM((1, hidden), F32),
            pltpu.VMEM((1, hidden), F32),
            pltpu.VMEM((1, hidden), F32),
            dma((5,)),
            dma((2, col_count)),
            dma((2, col_count)),
            dma((2, col_count)),
            dma((2, col_count)),
            dma((2, 3)),
            dma((2, 3)),
            dma((2, 3)),
            dma((2, 3)),
            dma((2, 3)),
            dma((2, 3)),
            dma((2,)),
            dma((2,)),
            dma((2, col_count - 1)),
            dma((2, col_count - 1)),
            dma((2,)),
            dma((2,)),
            dma((4,)),
        ],
        compiler_params=pltpu.CompilerParams(
            collective_id=0, has_side_effects=True, vmem_limit_bytes=44 * 2**20
        ),
        cost_estimate=pl.CostEstimate(
            flops=8 * rows * feats * hidden, bytes_accessed=8 * feats * hidden, transcendentals=rows * hidden
        ),
    )(tokens, out_grad, w_in, b_in, w_out)
    block_out, tokens_part, bias_grad, tok, og, act, hg = outs[:7]
    arrived = []
    for step, piece in enumerate(outs[7:], 1):
        to_peer = [(c, (c + step) % col_count) for c in range(col_count)]
        arrived.append(lax.ppermute(piece, "col", to_peer))
    whole_block = lambda i: (0, 0)
    w_in_grad, w_out_grad, block_out = pl.pallas_call(
        weight_kernel,
        grid=(hidden // TILE,),
        out_shape=[
            jax.ShapeDtypeStruct((feats, hidden), BF16),
            jax.ShapeDtypeStruct((hidden, feats), BF16),
            jax.ShapeDtypeStruct((tile_rows, feats), BF16),
        ],
        in_specs=[
            pl.BlockSpec((rows, feats), whole_block),
            pl.BlockSpec((rows, feats), whole_block),
            pl.BlockSpec((rows, TILE), lambda i: (0, i)),
            pl.BlockSpec((rows, TILE), lambda i: (0, i)),
            pl.BlockSpec((tile_rows, feats), whole_block),
        ],
        out_specs=[
            pl.BlockSpec((feats, TILE), lambda i: (0, i)),
            pl.BlockSpec((TILE, feats), lambda i: (i, 0)),
            pl.BlockSpec((tile_rows, feats), whole_block),
        ],
        scratch_shapes=[pltpu.VMEM((feats, rows), BF16)],
        compiler_params=pltpu.CompilerParams(vmem_limit_bytes=32 * 2**20),
        cost_estimate=pl.CostEstimate(
            flops=4 * rows * feats * hidden, bytes_accessed=4 * feats * hidden, transcendentals=0
        ),
    )(
        tok.reshape(rows, feats), og.reshape(rows, feats), act.reshape(rows, hidden), hg.reshape(rows, hidden),
        block_out,
    )
    tokens_grad = tokens_part
    for piece in arrived:
        tokens_grad = tokens_grad + piece.astype(F32)
    tokens_grad = tokens_grad.astype(BF16)
    return block_out, tokens_grad, w_in_grad, w_out_grad, bias_grad


def by_shape(mesh):
    def run(tokens, out_grad, w_in, b_in, w_out):
        depth_count = mesh.shape["depth"]
        fits = (
            mesh.shape["row"] == 4
            and depth_count == 2
            and mesh.shape["col"] > 1
            and tokens.shape[0] % 32 == 0
            and tokens.shape[1] % TILE == 0
            and w_in.shape[1] % (depth_count * TILE) == 0
        )
        if fits:
            return fused(mesh.shape["col"], tokens, out_grad, w_in, b_in, w_out)
        return local(tokens, out_grad, w_in, b_in, w_out)

    return run


def solution(mesh):
    return jax.shard_map(
        by_shape(mesh),
        mesh=mesh,
        in_specs=(
            P(("col", "depth"), "row"),
            P(("col", "depth"), "row"),
            P("row", "col"),
            P("col"),
            P("col", "row"),
        ),
        out_specs=(
            P(("col", "depth"), "row"),
            P(("col", "depth"), "row"),
            P("row", ("col", "depth")),
            P(("col", "depth"), "row"),
            P("col"),
        ),
        check_vma=False,
    )
```

```python
import functools

import jax
import jax.numpy as jnp
from jax import lax
from jax.experimental import pallas as pl
from jax.experimental.pallas import tpu as pltpu
from jax.sharding import PartitionSpec as P

root_coeff = 0.7978845608028654
cubic_coeff = 0.044715


def gelu_parts(pre_act):
    inner_arg = root_coeff * (pre_act + cubic_coeff * pre_act * pre_act * pre_act)
    tangent = jnp.tanh(inner_arg)
    gelu_value = 0.5 * pre_act * (1.0 + tangent)
    gelu_slope = 0.5 * (1.0 + tangent) + 0.5 * pre_act * (1.0 - tangent * tangent) * root_coeff * (
        1.0 + 3.0 * cubic_coeff * pre_act * pre_act
    )
    return (gelu_value, gelu_slope)


def right_transposed(left_side, right_side):
    return lax.dot_general(
        left_side, right_side, (((1,), (1,)), ((), ())), preferred_element_type=jnp.float32
    )


def left_transposed(left_side, right_side):
    return lax.dot_general(
        left_side, right_side, (((0,), (0,)), ((), ())), preferred_element_type=jnp.float32
    )


def depth_rows(gathered, col_count, depth_index, depth_count):
    tile_rows = gathered.shape[0] // (col_count * depth_count)
    shaped = gathered.reshape(col_count, depth_count, tile_rows, gathered.shape[1])
    picked = lax.dynamic_index_in_dim(shaped, depth_index, 1, keepdims=False)
    return picked.reshape(col_count * tile_rows, gathered.shape[1])


def local(tokens, out_grad, w_in, b_in, w_out):
    col_count = lax.axis_size("col")
    depth_count = lax.axis_size("depth")
    tile_rows = tokens.shape[0]
    part_cols = w_in.shape[1] // depth_count
    depth_index = lax.axis_index("depth")
    all_input, all_grad = (
        lax.all_gather(tokens, ("col", "depth"), axis=0, tiled=True),
        lax.all_gather(out_grad, ("col", "depth"), axis=0, tiled=True),
    )
    plane_input = depth_rows(all_input, col_count, depth_index, depth_count)
    plane_grad = depth_rows(all_grad, col_count, depth_index, depth_count)
    pre_sum = lax.psum_scatter(
        jnp.dot(plane_input, w_in, preferred_element_type=jnp.float32),
        "row",
        scatter_dimension=0,
        tiled=True,
    )
    pre_share = pre_sum + b_in
    gelu_value, gelu_slope = gelu_parts(pre_share)
    plane_act = lax.all_gather(gelu_value.astype(jnp.bfloat16), "row", axis=0, tiled=True)
    block_out = lax.psum_scatter(
        jnp.dot(plane_act, w_out, preferred_element_type=jnp.float32),
        "col",
        scatter_dimension=0,
        tiled=True,
    ).astype(jnp.bfloat16)
    grad_share = lax.psum_scatter(
        right_transposed(plane_grad, w_out), "row", scatter_dimension=0, tiled=True
    )
    pre_grad = grad_share * gelu_slope
    plane_hgrad = lax.all_gather(pre_grad.astype(jnp.bfloat16), "row", axis=0, tiled=True)
    b_in_grad = lax.psum(jnp.sum(pre_grad, axis=0), ("row", "depth"))
    tokens_grad = lax.psum_scatter(
        right_transposed(plane_hgrad, w_in), "col", scatter_dimension=0, tiled=True
    ).astype(jnp.bfloat16)
    act_parts = lax.all_to_all(
        plane_act.reshape(col_count, tile_rows, w_in.shape[1]),
        "depth",
        split_axis=2,
        concat_axis=1,
        tiled=True,
    )
    act_parts = act_parts.reshape(-1, part_cols)
    hgrad_parts = lax.all_to_all(
        plane_hgrad.reshape(col_count, tile_rows, w_in.shape[1]),
        "depth",
        split_axis=2,
        concat_axis=1,
        tiled=True,
    )
    hgrad_parts = hgrad_parts.reshape(-1, part_cols)
    w_in_grad = left_transposed(all_input, hgrad_parts)
    w_out_grad = left_transposed(act_parts, all_grad)
    return (
        block_out,
        tokens_grad,
        w_in_grad.astype(jnp.bfloat16),
        w_out_grad.astype(jnp.bfloat16),
        b_in_grad,
    )


MESH = pl.DeviceIdType.MESH
TILE = 256
BF16 = jnp.bfloat16
F32 = jnp.float32


def block_kernel(
    col_count,
    tokens_ref, grad_ref, w_in_ref, bias_ref, w_out_ref,
    *refs,
):
    away = col_count - 1
    out_ref, tgrad_ref, bgrad_ref, tok_out, og_out, act_out, hg_out = refs[:7]
    tgrad_away = refs[7:7 + away]
    (
    tok, og, w_in, w_out, bias, b_all, part, part16, core_in, chip16, y_in, act, hg, slope,
    x_out, x_in, z_sum, z_out, z_in, b_acc, b_core, b_own, b_x,
    local_sem, z_ssem, z_rsem, x_ssem, x_rsem, c_ssem, c_rsem, y_ssem, y_rsem,
    a_ssem, a_rsem, rx_ssem, rx_rsem, rz_ssem, rz_rsem, b_ssem, b_rsem, out_sem,
    ) = refs[7 + away:]
    row = lax.axis_index("row")
    col = lax.axis_index("col")
    depth = lax.axis_index("depth")
    core = lax.rem(row, 2)
    core_peer = {"row": row + 1 - 2 * core}
    y_peer = {"row": lax.rem(row + 2, 4)}
    x_peer = {"depth": 1 - depth}
    hidden = w_in.shape[1]
    feats = w_in.shape[0]
    half = part.shape[4]

    def z_peer(step):
        return {"col": lax.rem(col + step, col_count)}

    def remote(src, dst, ssem, rsem, peer):
        return pltpu.make_async_remote_copy(
            src_ref=src, dst_ref=dst, send_sem=ssem, recv_sem=rsem, device_id=peer, device_id_type=MESH
        )

    base = pl.multiple_of(depth * hidden, 128)
    locals_ = [
        pltpu.make_async_copy(tokens_ref, tok.at[0, 0], local_sem.at[0]),
        pltpu.make_async_copy(w_in_ref.at[:, pl.ds(base, hidden)], w_in, local_sem.at[1]),
        pltpu.make_async_copy(grad_ref, og.at[0, 0], local_sem.at[2]),
        pltpu.make_async_copy(w_out_ref.at[pl.ds(base, hidden), :], w_out, local_sem.at[3]),
        pltpu.make_async_copy(bias_ref, bias, local_sem.at[4]),
    ]
    for copy in locals_:
        copy.start()

    barrier = pltpu.get_barrier_semaphore()
    peers = [z_peer(step) for step in range(1, col_count)] + [x_peer, y_peer, core_peer]
    for peer in peers:
        pl.semaphore_signal(barrier, inc=1, device_id=peer, device_id_type=MESH)
    pl.semaphore_wait(barrier, len(peers))

    sends = []

    def start(copy):
        copy.start()
        sends.append(copy)
        return copy

    def pair_start(which, src, dst):
        start(remote(src, dst.at[1, 0], x_ssem.at[which, 0], x_rsem.at[which, 0], x_peer))

    def line_start(which, src, dst):
        for step in range(1, col_count):
            start(remote(src, dst.at[0, step], z_ssem.at[which, step], z_rsem.at[which, step], z_peer(step)))

    def gather_own(which, dst):
        for step in range(1, col_count):
            block = dst.at[0, step]
            remote(block, block, z_ssem.at[which, step], z_rsem.at[which, step], z_peer(step)).wait_recv()
            start(remote(block, dst.at[1, step], x_ssem.at[which, step], x_rsem.at[which, step], x_peer))

    def other_wait(which, dst, step):
        block = dst.at[1, step]
        remote(block, block, x_ssem.at[which, step], x_rsem.at[which, step], x_peer).wait_recv()

    def gather_other(which, dst):
        for step in range(1, col_count):
            other_wait(which, dst, step)

    def tile_of(i):
        return pl.ds(pl.multiple_of(i * TILE, TILE), TILE)

    def cut(group):
        return pl.ds(group[1][0], len(group[1])), pl.ds(group[2][0], len(group[2]))

    def rows_of(buf, group):
        value = buf[(*cut(group),)]
        return value.reshape(-1, value.shape[-1])

    def places(group):
        return [(chunk, s) for chunk in group[1] for s in group[2]]

    def product(which, group, multiply, parts):
        @pl.loop(0, hidden // TILE, unroll=True)
        def _(i):
            at = tile_of(i)
            value = multiply(rows_of(og if which else tok, group), at)
            for n, (chunk, s) in enumerate(places(group)):
                for k in range(2):
                    piece = value[(2 * n + k) * half:(2 * n + k + 1) * half]
                    part[which, k, chunk, s, :, at] = piece
                    part16[which, k, chunk, s, :, at] = piece.astype(BF16)

        for group in parts:
            start(remote(
                part16.at[(which, 1 - core, *cut(group))], core_in.at[(which, *cut(group))],
                c_ssem.at[which, group[0]], c_rsem.at[which, group[0]], core_peer,
            ))

    def chip_sum(which, group):
        landed = core_in.at[(which, *cut(group))]
        remote(landed, landed, c_ssem.at[which, group[0]], c_rsem.at[which, group[0]], core_peer).wait_recv()

        @pl.loop(0, hidden // TILE, unroll=True)
        def _(i):
            at = tile_of(i)
            for chunk, s in places(group):
                total = part[which, core, chunk, s, :, at] + core_in[which, chunk, s, :, at].astype(F32)
                chip16[which, chunk, s, :, at] = total.astype(BF16)

        start(remote(
            chip16.at[(which, *cut(group))], y_in.at[(which, *cut(group))],
            y_ssem.at[which, group[0]], y_rsem.at[which, group[0]], y_peer,
        ))

    def y_wait(which, group):
        landed = y_in.at[(which, *cut(group))]
        remote(landed, landed, y_ssem.at[which, group[0]], y_rsem.at[which, group[0]], y_peer).wait_recv()

    def row_sum(which, chunk, s, at):
        return chip16[which, chunk, s, :, at].astype(F32) + y_in[which, chunk, s, :, at].astype(F32)

    def share(which, group, buf, whose):
        piece = buf.at[(*cut(group), whose)]
        return remote(piece, piece, a_ssem.at[which, group[0]], a_rsem.at[which, group[0]], core_peer)

    def activate(group):
        y_wait(0, group)

        @pl.loop(0, hidden // TILE, unroll=True)
        def _(i):
            at = tile_of(i)
            bias_here = b_all[:, pl.ds(pl.multiple_of(depth * hidden + i * TILE, 128), TILE)]
            for chunk, s in places(group):
                value, slope_here = gelu_parts(row_sum(0, chunk, s, at) + bias_here)
                act[chunk, s, core, :, at] = value.astype(BF16)
                slope[chunk, s, :, at] = slope_here

        start(share(0, group, act, core))

    def hidden_grad(group, fresh):
        y_wait(1, group)

        @pl.loop(0, hidden // TILE, unroll=True)
        def _(i):
            at = tile_of(i)
            total = None if fresh else b_acc[:, at]
            for chunk, s in places(group):
                pre_grad = row_sum(1, chunk, s, at) * slope[chunk, s, :, at]
                hg[chunk, s, core, :, at] = pre_grad.astype(BF16)
                here = jnp.sum(pre_grad, axis=0, keepdims=True)
                total = here if total is None else total + here
            b_acc[:, at] = total

        start(share(1, group, hg, core))

    def project(which, chunk, buf, multiply):
        tile_rows = x_out.shape[2]

        @pl.loop(0, feats // TILE, unroll=True)
        def _(i):
            at = tile_of(i)
            value = multiply(rows_of(buf, (0, (chunk,), range(col_count))), at)
            for c in range(col_count):
                piece = value[c * tile_rows:(c + 1) * tile_rows]
                if chunk == 1:
                    x_out[which, c, :, at] = piece.astype(BF16)
                else:
                    z_sum[which, c, :, at] = piece

        if chunk == 1:
            start(remote(x_out.at[which], x_in.at[which], rx_ssem.at[which], rx_rsem.at[which], x_peer))

    def plane_sum(which):
        landed = x_in.at[which]
        remote(landed, landed, rx_ssem.at[which], rx_rsem.at[which], x_peer).wait_recv()
        for c in range(col_count):
            total = z_sum[which, c] + x_in[which, c].astype(F32)
            z_sum[which, c] = total
            z_out[which, c] = total.astype(BF16)
        for step in range(1, col_count):
            start(remote(
                z_out.at[which, col_count - step], z_in.at[which, step - 1],
                rz_ssem.at[which, step - 1], rz_rsem.at[which, step - 1], z_peer(step),
            ))

    def final_sum(which, result):
        for step in range(1, col_count):
            landed = z_in.at[which, step - 1]
            remote(
                landed, landed, rz_ssem.at[which, step - 1], rz_rsem.at[which, step - 1], z_peer(step)
            ).wait_recv()
        total = z_sum[which, 0]
        for step in range(1, col_count):
            total = total + z_in[which, step - 1].astype(F32)
        result[...] = total.astype(BF16)

    def keep(which, src, dst):
        copy = pltpu.make_async_copy(src, dst, out_sem.at[which])
        copy.start()
        return copy

    def pre_tile(value, at):
        return jnp.dot(value, w_in[:, at], preferred_element_type=F32)

    def back_tile(value, at):
        return right_transposed(value, w_out[at, :])

    steps = range(1, col_count)
    pair, far, near = (0, (0, 1), (0,)), (1, (1,), steps), (2, (0,), steps)
    rest = (None, (0, 1), steps)

    pair_start(0, tokens_ref, tok)
    line_start(0, tokens_ref, tok)
    pair_start(1, grad_ref, og)
    locals_[4].wait()
    b_all[...] = bias[...].reshape(1, 2 * hidden)
    locals_[0].wait()
    locals_[1].wait()
    other_wait(0, tok, 0)
    product(0, pair, pre_tile, [pair])
    locals_[2].wait()
    locals_[3].wait()
    other_wait(1, og, 0)
    product(1, pair, back_tile, [pair])
    line_start(1, grad_ref, og)
    chip_sum(0, pair)
    chip_sum(1, pair)
    gather_own(0, tok)
    gather_other(0, tok)
    product(0, rest, pre_tile, [far, near])
    kept = [keep(0, tok, tok_out)]
    chip_sum(0, far)
    chip_sum(0, near)
    gather_own(1, og)
    activate(pair)
    gather_other(1, og)
    kept.append(keep(1, og, og_out))
    product(1, rest, back_tile, [far, near])
    activate(far)
    chip_sum(1, far)
    chip_sum(1, near)
    share(0, pair, act, 1 - core).wait_recv()
    share(0, far, act, 1 - core).wait_recv()

    def forward(value, at):
        return jnp.dot(value, w_out[:, at], preferred_element_type=F32)

    def backward(value, at):
        return right_transposed(value, w_in[at, :])

    project(0, 1, act, forward)
    activate(near)
    hidden_grad(pair, True)
    share(0, near, act, 1 - core).wait_recv()
    kept.append(keep(2, act, act_out))
    project(0, 0, act, forward)
    hidden_grad(far, False)
    share(1, pair, hg, 1 - core).wait_recv()
    share(1, far, hg, 1 - core).wait_recv()
    project(1, 1, hg, backward)
    plane_sum(0)
    hidden_grad(near, False)
    start(remote(b_acc, b_core, b_ssem.at[0], b_rsem.at[0], core_peer))
    share(1, near, hg, 1 - core).wait_recv()
    kept.append(keep(3, hg, hg_out))
    remote(b_core, b_core, b_ssem.at[0], b_rsem.at[0], core_peer).wait_recv()
    b_own[...] = b_acc[...] + b_core[...]
    start(remote(b_own, b_x, b_ssem.at[1], b_rsem.at[1], x_peer))
    project(1, 0, hg, backward)
    final_sum(0, out_ref)
    landed = x_in.at[1]
    remote(landed, landed, rx_ssem.at[1], rx_rsem.at[1], x_peer).wait_recv()
    tgrad_ref[...] = z_sum[1, 0] + x_in[1, 0].astype(F32)
    for step in range(1, col_count):
        total = z_sum[1, col_count - step] + x_in[1, col_count - step].astype(F32)
        tgrad_away[step - 1][...] = total.astype(BF16)
    remote(b_x, b_x, b_ssem.at[1], b_rsem.at[1], x_peer).wait_recv()
    b_all[:, pl.ds(base, hidden)] = b_own[...]
    b_all[:, pl.ds(pl.multiple_of((1 - depth) * hidden, 128), hidden)] = b_x[...]
    bgrad_ref[...] = b_all[...].reshape(2 * hidden)
    for copy in kept:
        copy.wait()
    for copy in sends:
        copy.wait_send()


def weight_kernel(
    tok_ref, og_ref, act_ref, hg_ref, out_ref, bgrad_ref,
    w_in_grad_ref, w_out_grad_ref, out_again, bgrad_again, tok_turned,
):
    @pl.when(pl.program_id(0) == 0)
    def _():
        tok_turned[...] = tok_ref[...].T
        out_again[...] = out_ref[...]
        bgrad_again[...] = bgrad_ref[...]

    w_in_grad_ref[...] = jnp.dot(tok_turned[...], hg_ref[...], preferred_element_type=F32).astype(BF16)
    w_out_grad_ref[...] = left_transposed(act_ref[...], og_ref[...]).astype(BF16)


def fused(col_count, tokens, out_grad, w_in, b_in, w_out):
    tile_rows, feats = tokens.shape
    hidden = w_in.shape[1] // 2
    plane = col_count * tile_rows
    half = tile_rows // 2
    rows = 2 * plane
    anywhere = pl.BlockSpec(memory_space=pltpu.HBM)
    vmem = pl.BlockSpec(memory_space=pltpu.VMEM)
    dma = pltpu.SemaphoreType.DMA
    outs = pl.pallas_call(
        functools.partial(block_kernel, col_count),
        out_shape=[
            jax.ShapeDtypeStruct((tile_rows, feats), BF16),
            jax.ShapeDtypeStruct((tile_rows, feats), F32),
            jax.ShapeDtypeStruct((2 * hidden,), F32),
            jax.ShapeDtypeStruct((2, col_count, tile_rows, feats), BF16),
            jax.ShapeDtypeStruct((2, col_count, tile_rows, feats), BF16),
            jax.ShapeDtypeStruct((2, col_count, 2, half, hidden), BF16),
            jax.ShapeDtypeStruct((2, col_count, 2, half, hidden), BF16),
        ] + [jax.ShapeDtypeStruct((tile_rows, feats), BF16)] * (col_count - 1),
        in_specs=[anywhere] * 5,
        out_specs=[vmem, vmem, vmem, anywhere, anywhere, anywhere, anywhere] + [vmem] * (col_count - 1),
        scratch_shapes=[
            pltpu.VMEM((2, col_count, tile_rows, feats), BF16),
            pltpu.VMEM((2, col_count, tile_rows, feats), BF16),
            pltpu.VMEM((feats, hidden), BF16),
            pltpu.VMEM((hidden, feats), BF16),
            pltpu.VMEM((2 * hidden,), F32),
            pltpu.VMEM((1, 2 * hidden), F32),
            pltpu.VMEM((2, 2, 2, col_count, half, hidden), F32),
            pltpu.VMEM((2, 2, 2, col_count, half, hidden), BF16),
            pltpu.VMEM((2, 2, col_count, half, hidden), BF16),
            pltpu.VMEM((2, 2, col_count, half, hidden), BF16),
            pltpu.VMEM((2, 2, col_count, half, hidden), BF16),
            pltpu.VMEM((2, col_count, 2, half, hidden), BF16),
            pltpu.VMEM((2, col_count, 2, half, hidden), BF16),
            pltpu.VMEM((2, col_count, half, hidden), F32),
            pltpu.VMEM((2, col_count, tile_rows, feats), BF16),
            pltpu.VMEM((2, col_count, tile_rows, feats), BF16),
            pltpu.VMEM((2, col_count, tile_rows, feats), F32),
            pltpu.VMEM((2, col_count, tile_rows, feats), BF16),
            pltpu.VMEM((2, col_count - 1, tile_rows, feats), BF16),
            pltpu.VMEM((1, hidden), F32),
            pltpu.VMEM((1, hidden), F32),
            pltpu.VMEM((1, hidden), F32),
            pltpu.VMEM((1, hidden), F32),
            dma((5,)),
            dma((2, col_count)),
            dma((2, col_count)),
            dma((2, col_count)),
            dma((2, col_count)),
            dma((2, 3)),
            dma((2, 3)),
            dma((2, 3)),
            dma((2, 3)),
            dma((2, 3)),
            dma((2, 3)),
            dma((2,)),
            dma((2,)),
            dma((2, col_count - 1)),
            dma((2, col_count - 1)),
            dma((2,)),
            dma((2,)),
            dma((4,)),
        ],
        compiler_params=pltpu.CompilerParams(
            collective_id=0, has_side_effects=True, vmem_limit_bytes=64 * 2**20
        ),
        cost_estimate=pl.CostEstimate(
            flops=8 * rows * feats * hidden, bytes_accessed=8 * feats * hidden, transcendentals=rows * hidden
        ),
    )(tokens, out_grad, w_in, b_in, w_out)
    block_out, tokens_part, bias_grad, tok, og, act, hg = outs[:7]
    arrived = []
    for step, piece in enumerate(outs[7:], 1):
        to_peer = [(c, (c + step) % col_count) for c in range(col_count)]
        arrived.append(lax.ppermute(piece, "col", to_peer))
    whole_block = lambda i: (0, 0)
    w_in_grad, w_out_grad, block_out, bias_grad = pl.pallas_call(
        weight_kernel,
        grid=(hidden // TILE,),
        out_shape=[
            jax.ShapeDtypeStruct((feats, hidden), BF16),
            jax.ShapeDtypeStruct((hidden, feats), BF16),
            jax.ShapeDtypeStruct((tile_rows, feats), BF16),
            jax.ShapeDtypeStruct((2 * hidden,), F32),
        ],
        in_specs=[
            pl.BlockSpec((rows, feats), whole_block),
            pl.BlockSpec((rows, feats), whole_block),
            pl.BlockSpec((rows, TILE), lambda i: (0, i)),
            pl.BlockSpec((rows, TILE), lambda i: (0, i)),
            pl.BlockSpec((tile_rows, feats), whole_block),
            pl.BlockSpec((2 * hidden,), lambda i: (0,)),
        ],
        out_specs=[
            pl.BlockSpec((feats, TILE), lambda i: (0, i)),
            pl.BlockSpec((TILE, feats), lambda i: (i, 0)),
            pl.BlockSpec((tile_rows, feats), whole_block),
            pl.BlockSpec((2 * hidden,), lambda i: (0,)),
        ],
        scratch_shapes=[pltpu.VMEM((feats, rows), BF16)],
        compiler_params=pltpu.CompilerParams(vmem_limit_bytes=64 * 2**20),
        cost_estimate=pl.CostEstimate(
            flops=4 * rows * feats * hidden, bytes_accessed=4 * feats * hidden, transcendentals=0
        ),
    )(
        tok.reshape(rows, feats), og.reshape(rows, feats), act.reshape(rows, hidden), hg.reshape(rows, hidden),
        block_out, bias_grad,
    )
    tokens_grad = tokens_part
    for piece in arrived:
        tokens_grad = tokens_grad + piece.astype(F32)
    tokens_grad = tokens_grad.astype(BF16)
    return block_out, tokens_grad, w_in_grad, w_out_grad, bias_grad


def by_shape(mesh):
    def run(tokens, out_grad, w_in, b_in, w_out):
        depth_count = mesh.shape["depth"]
        fits = (
            mesh.shape["row"] == 4
            and depth_count == 2
            and mesh.shape["col"] > 1
            and tokens.shape[0] % 32 == 0
            and tokens.shape[1] % TILE == 0
            and w_in.shape[1] % (depth_count * TILE) == 0
        )
        if fits:
            return fused(mesh.shape["col"], tokens, out_grad, w_in, b_in, w_out)
        return local(tokens, out_grad, w_in, b_in, w_out)

    return run


def solution(mesh):
    return jax.shard_map(
        by_shape(mesh),
        mesh=mesh,
        in_specs=(
            P(("col", "depth"), "row"),
            P(("col", "depth"), "row"),
            P("row", "col"),
            P("col"),
            P("col", "row"),
        ),
        out_specs=(
            P(("col", "depth"), "row"),
            P(("col", "depth"), "row"),
            P("row", ("col", "depth")),
            P(("col", "depth"), "row"),
            P("col"),
        ),
        check_vma=False,
    )
```

```python
import functools

import jax
import jax.numpy as jnp
from jax import lax
from jax.experimental import pallas as pl
from jax.experimental.pallas import tpu as pltpu
from jax.sharding import PartitionSpec as P

root_coeff = 0.7978845608028654
cubic_coeff = 0.044715


def gelu_parts(pre_act):
    inner_arg = root_coeff * (pre_act + cubic_coeff * pre_act * pre_act * pre_act)
    tangent = jnp.tanh(inner_arg)
    gelu_value = 0.5 * pre_act * (1.0 + tangent)
    gelu_slope = 0.5 * (1.0 + tangent) + 0.5 * pre_act * (1.0 - tangent * tangent) * root_coeff * (
        1.0 + 3.0 * cubic_coeff * pre_act * pre_act
    )
    return (gelu_value, gelu_slope)


def right_transposed(left_side, right_side):
    return lax.dot_general(
        left_side, right_side, (((1,), (1,)), ((), ())), preferred_element_type=jnp.float32
    )


def left_transposed(left_side, right_side):
    return lax.dot_general(
        left_side, right_side, (((0,), (0,)), ((), ())), preferred_element_type=jnp.float32
    )


def depth_rows(gathered, col_count, depth_index, depth_count):
    tile_rows = gathered.shape[0] // (col_count * depth_count)
    shaped = gathered.reshape(col_count, depth_count, tile_rows, gathered.shape[1])
    picked = lax.dynamic_index_in_dim(shaped, depth_index, 1, keepdims=False)
    return picked.reshape(col_count * tile_rows, gathered.shape[1])


def local(tokens, out_grad, w_in, b_in, w_out):
    col_count = lax.axis_size("col")
    depth_count = lax.axis_size("depth")
    tile_rows = tokens.shape[0]
    part_cols = w_in.shape[1] // depth_count
    depth_index = lax.axis_index("depth")
    all_input, all_grad = (
        lax.all_gather(tokens, ("col", "depth"), axis=0, tiled=True),
        lax.all_gather(out_grad, ("col", "depth"), axis=0, tiled=True),
    )
    plane_input = depth_rows(all_input, col_count, depth_index, depth_count)
    plane_grad = depth_rows(all_grad, col_count, depth_index, depth_count)
    pre_sum = lax.psum_scatter(
        jnp.dot(plane_input, w_in, preferred_element_type=jnp.float32),
        "row",
        scatter_dimension=0,
        tiled=True,
    )
    pre_share = pre_sum + b_in
    gelu_value, gelu_slope = gelu_parts(pre_share)
    plane_act = lax.all_gather(gelu_value.astype(jnp.bfloat16), "row", axis=0, tiled=True)
    block_out = lax.psum_scatter(
        jnp.dot(plane_act, w_out, preferred_element_type=jnp.float32),
        "col",
        scatter_dimension=0,
        tiled=True,
    ).astype(jnp.bfloat16)
    grad_share = lax.psum_scatter(
        right_transposed(plane_grad, w_out), "row", scatter_dimension=0, tiled=True
    )
    pre_grad = grad_share * gelu_slope
    plane_hgrad = lax.all_gather(pre_grad.astype(jnp.bfloat16), "row", axis=0, tiled=True)
    b_in_grad = lax.psum(jnp.sum(pre_grad, axis=0), ("row", "depth"))
    tokens_grad = lax.psum_scatter(
        right_transposed(plane_hgrad, w_in), "col", scatter_dimension=0, tiled=True
    ).astype(jnp.bfloat16)
    act_parts = lax.all_to_all(
        plane_act.reshape(col_count, tile_rows, w_in.shape[1]),
        "depth",
        split_axis=2,
        concat_axis=1,
        tiled=True,
    )
    act_parts = act_parts.reshape(-1, part_cols)
    hgrad_parts = lax.all_to_all(
        plane_hgrad.reshape(col_count, tile_rows, w_in.shape[1]),
        "depth",
        split_axis=2,
        concat_axis=1,
        tiled=True,
    )
    hgrad_parts = hgrad_parts.reshape(-1, part_cols)
    w_in_grad = left_transposed(all_input, hgrad_parts)
    w_out_grad = left_transposed(act_parts, all_grad)
    return (
        block_out,
        tokens_grad,
        w_in_grad.astype(jnp.bfloat16),
        w_out_grad.astype(jnp.bfloat16),
        b_in_grad,
    )


MESH = pl.DeviceIdType.MESH
TILE = 256
BF16 = jnp.bfloat16
F32 = jnp.float32


def block_kernel(
    col_count,
    tokens_ref, grad_ref, w_in_ref, bias_ref, w_out_ref,
    *refs,
):
    away = col_count - 1
    out_ref, tgrad_ref, bgrad_ref, tok_out, og_out, act_out, hg_out = refs[:7]
    tgrad_away = refs[7:7 + away]
    (
    tok, og, w_in, w_out, bias, b_all, part, part16, core_in, chip16, y_in, act, hg, slope,
    x_out, x_in, z_sum, z_out, z_in, b_acc, b_core, b_own, b_x,
    local_sem, z_ssem, z_rsem, x_ssem, x_rsem, c_ssem, c_rsem, y_ssem, y_rsem,
    a_ssem, a_rsem, rx_ssem, rx_rsem, rz_ssem, rz_rsem, b_ssem, b_rsem, out_sem,
    ) = refs[7 + away:]
    row = lax.axis_index("row")
    col = lax.axis_index("col")
    depth = lax.axis_index("depth")
    core = lax.rem(row, 2)
    core_peer = {"row": row + 1 - 2 * core}
    y_peer = {"row": lax.rem(row + 2, 4)}
    x_peer = {"depth": 1 - depth}
    hidden = w_in.shape[1]
    feats = w_in.shape[0]
    half = part.shape[4]

    def z_peer(step):
        return {"col": lax.rem(col + step, col_count)}

    def remote(src, dst, ssem, rsem, peer):
        return pltpu.make_async_remote_copy(
            src_ref=src, dst_ref=dst, send_sem=ssem, recv_sem=rsem, device_id=peer, device_id_type=MESH
        )

    base = pl.multiple_of(depth * hidden, 128)
    locals_ = [
        pltpu.make_async_copy(tokens_ref, tok.at[0, 0], local_sem.at[0]),
        pltpu.make_async_copy(w_in_ref.at[:, pl.ds(base, hidden)], w_in, local_sem.at[1]),
        pltpu.make_async_copy(grad_ref, og.at[0, 0], local_sem.at[2]),
        pltpu.make_async_copy(w_out_ref.at[pl.ds(base, hidden), :], w_out, local_sem.at[3]),
        pltpu.make_async_copy(bias_ref, bias, local_sem.at[4]),
    ]
    for copy in locals_:
        copy.start()

    barrier = pltpu.get_barrier_semaphore()
    peers = [z_peer(step) for step in range(1, col_count)] + [x_peer, y_peer, core_peer]
    for peer in peers:
        pl.semaphore_signal(barrier, inc=1, device_id=peer, device_id_type=MESH)
    pl.semaphore_wait(barrier, len(peers))

    sends = []

    def start(copy):
        copy.start()
        sends.append(copy)
        return copy

    def pair_start(which, src, dst):
        start(remote(src, dst.at[1, 0], x_ssem.at[which, 0], x_rsem.at[which, 0], x_peer))

    def line_start(which, src, dst):
        for step in range(1, col_count):
            start(remote(src, dst.at[0, step], z_ssem.at[which, step], z_rsem.at[which, step], z_peer(step)))

    def gather_own(which, dst):
        for step in range(1, col_count):
            block = dst.at[0, step]
            remote(block, block, z_ssem.at[which, step], z_rsem.at[which, step], z_peer(step)).wait_recv()
            start(remote(block, dst.at[1, step], x_ssem.at[which, step], x_rsem.at[which, step], x_peer))

    def other_wait(which, dst, step):
        block = dst.at[1, step]
        remote(block, block, x_ssem.at[which, step], x_rsem.at[which, step], x_peer).wait_recv()

    def gather_other(which, dst):
        for step in range(1, col_count):
            other_wait(which, dst, step)

    def tile_of(i):
        return pl.ds(pl.multiple_of(i * TILE, TILE), TILE)

    def cut(group):
        return pl.ds(group[1][0], len(group[1])), pl.ds(group[2][0], len(group[2]))

    def rows_of(buf, group):
        value = buf[(*cut(group),)]
        return value.reshape(-1, value.shape[-1])

    def places(group):
        return [(chunk, s) for chunk in group[1] for s in group[2]]

    def product(which, group, multiply, parts):
        @pl.loop(0, hidden // TILE, unroll=True)
        def _(i):
            at = tile_of(i)
            value = multiply(rows_of(og if which else tok, group), at)
            for n, (chunk, s) in enumerate(places(group)):
                for k in range(2):
                    piece = value[(2 * n + k) * half:(2 * n + k + 1) * half]
                    part[which, k, chunk, s, :, at] = piece
                    part16[which, k, chunk, s, :, at] = piece.astype(BF16)

        for group in parts:
            start(remote(
                part16.at[(which, 1 - core, *cut(group))], core_in.at[(which, *cut(group))],
                c_ssem.at[which, group[0]], c_rsem.at[which, group[0]], core_peer,
            ))

    def chip_sum(which, group):
        landed = core_in.at[(which, *cut(group))]
        remote(landed, landed, c_ssem.at[which, group[0]], c_rsem.at[which, group[0]], core_peer).wait_recv()

        @pl.loop(0, hidden // TILE, unroll=True)
        def _(i):
            at = tile_of(i)
            for chunk, s in places(group):
                total = part[which, core, chunk, s, :, at] + core_in[which, chunk, s, :, at].astype(F32)
                chip16[which, chunk, s, :, at] = total.astype(BF16)

        start(remote(
            chip16.at[(which, *cut(group))], y_in.at[(which, *cut(group))],
            y_ssem.at[which, group[0]], y_rsem.at[which, group[0]], y_peer,
        ))

    def y_wait(which, group):
        landed = y_in.at[(which, *cut(group))]
        remote(landed, landed, y_ssem.at[which, group[0]], y_rsem.at[which, group[0]], y_peer).wait_recv()

    def row_sum(which, chunk, s, at):
        return chip16[which, chunk, s, :, at].astype(F32) + y_in[which, chunk, s, :, at].astype(F32)

    def share(which, group, buf, whose):
        piece = buf.at[(*cut(group), whose)]
        return remote(piece, piece, a_ssem.at[which, group[0]], a_rsem.at[which, group[0]], core_peer)

    def activate(group):
        y_wait(0, group)

        @pl.loop(0, hidden // TILE, unroll=True)
        def _(i):
            at = tile_of(i)
            bias_here = b_all[:, pl.ds(pl.multiple_of(depth * hidden + i * TILE, 128), TILE)]
            for chunk, s in places(group):
                value, slope_here = gelu_parts(row_sum(0, chunk, s, at) + bias_here)
                act[chunk, s, core, :, at] = value.astype(BF16)
                slope[chunk, s, :, at] = slope_here

        start(share(0, group, act, core))

    def hidden_grad(group, fresh):
        y_wait(1, group)

        @pl.loop(0, hidden // TILE, unroll=True)
        def _(i):
            at = tile_of(i)
            total = None if fresh else b_acc[:, at]
            for chunk, s in places(group):
                pre_grad = row_sum(1, chunk, s, at) * slope[chunk, s, :, at]
                hg[chunk, s, core, :, at] = pre_grad.astype(BF16)
                here = jnp.sum(pre_grad, axis=0, keepdims=True)
                total = here if total is None else total + here
            b_acc[:, at] = total

        start(share(1, group, hg, core))

    def project(which, chunk, buf, multiply):
        tile_rows = x_out.shape[2]

        @pl.loop(0, feats // TILE, unroll=True)
        def _(i):
            at = tile_of(i)
            value = multiply(rows_of(buf, (0, (chunk,), range(col_count))), at)
            for c in range(col_count):
                piece = value[c * tile_rows:(c + 1) * tile_rows]
                if chunk == 1:
                    x_out[which, c, :, at] = piece.astype(BF16)
                else:
                    z_sum[which, c, :, at] = piece

        if chunk == 1:
            start(remote(x_out.at[which], x_in.at[which], rx_ssem.at[which], rx_rsem.at[which], x_peer))

    def plane_sum(which):
        landed = x_in.at[which]
        remote(landed, landed, rx_ssem.at[which], rx_rsem.at[which], x_peer).wait_recv()
        for c in range(col_count):
            total = z_sum[which, c] + x_in[which, c].astype(F32)
            z_sum[which, c] = total
            z_out[which, c] = total.astype(BF16)
        for step in range(1, col_count):
            start(remote(
                z_out.at[which, col_count - step], z_in.at[which, step - 1],
                rz_ssem.at[which, step - 1], rz_rsem.at[which, step - 1], z_peer(step),
            ))

    def final_sum(which, result):
        for step in range(1, col_count):
            landed = z_in.at[which, step - 1]
            remote(
                landed, landed, rz_ssem.at[which, step - 1], rz_rsem.at[which, step - 1], z_peer(step)
            ).wait_recv()
        total = z_sum[which, 0]
        for step in range(1, col_count):
            total = total + z_in[which, step - 1].astype(F32)
        result[...] = total.astype(BF16)

    def keep(which, src, dst):
        copy = pltpu.make_async_copy(src, dst, out_sem.at[which])
        copy.start()
        return copy

    def pre_tile(value, at):
        return jnp.dot(value, w_in[:, at], preferred_element_type=F32)

    def back_tile(value, at):
        return right_transposed(value, w_out[at, :])

    steps = range(1, col_count)
    pair, far, near = (0, (0, 1), (0,)), (1, (1,), steps), (2, (0,), steps)
    rest = (None, (0, 1), steps)

    pair_start(0, tokens_ref, tok)
    line_start(0, tokens_ref, tok)
    pair_start(1, grad_ref, og)
    locals_[4].wait()
    b_all[...] = bias[...].reshape(1, 2 * hidden)
    locals_[0].wait()
    locals_[1].wait()
    other_wait(0, tok, 0)
    product(0, pair, pre_tile, [pair])
    locals_[2].wait()
    locals_[3].wait()
    other_wait(1, og, 0)
    product(1, pair, back_tile, [pair])
    line_start(1, grad_ref, og)
    chip_sum(0, pair)
    chip_sum(1, pair)
    gather_own(0, tok)
    gather_other(0, tok)
    product(0, rest, pre_tile, [far, near])
    kept = [keep(0, tok, tok_out)]
    chip_sum(0, far)
    chip_sum(0, near)
    gather_own(1, og)
    activate(pair)
    gather_other(1, og)
    kept.append(keep(1, og, og_out))
    product(1, rest, back_tile, [far, near])
    activate(far)
    chip_sum(1, far)
    chip_sum(1, near)
    share(0, pair, act, 1 - core).wait_recv()
    share(0, far, act, 1 - core).wait_recv()

    def forward(value, at):
        return jnp.dot(value, w_out[:, at], preferred_element_type=F32)

    def backward(value, at):
        return right_transposed(value, w_in[at, :])

    project(0, 1, act, forward)
    activate(near)
    hidden_grad(pair, True)
    share(0, near, act, 1 - core).wait_recv()
    kept.append(keep(2, act, act_out))
    project(0, 0, act, forward)
    hidden_grad(far, False)
    share(1, pair, hg, 1 - core).wait_recv()
    share(1, far, hg, 1 - core).wait_recv()
    project(1, 1, hg, backward)
    plane_sum(0)
    hidden_grad(near, False)
    start(remote(b_acc, b_core, b_ssem.at[0], b_rsem.at[0], core_peer))
    share(1, near, hg, 1 - core).wait_recv()
    kept.append(keep(3, hg, hg_out))
    remote(b_core, b_core, b_ssem.at[0], b_rsem.at[0], core_peer).wait_recv()
    b_own[...] = b_acc[...] + b_core[...]
    start(remote(b_own, b_x, b_ssem.at[1], b_rsem.at[1], x_peer))
    project(1, 0, hg, backward)
    final_sum(0, out_ref)
    landed = x_in.at[1]
    remote(landed, landed, rx_ssem.at[1], rx_rsem.at[1], x_peer).wait_recv()
    tgrad_ref[...] = z_sum[1, 0] + x_in[1, 0].astype(F32)
    for step in range(1, col_count):
        total = z_sum[1, col_count - step] + x_in[1, col_count - step].astype(F32)
        tgrad_away[step - 1][...] = total.astype(BF16)
    remote(b_x, b_x, b_ssem.at[1], b_rsem.at[1], x_peer).wait_recv()
    b_all[:, pl.ds(base, hidden)] = b_own[...]
    b_all[:, pl.ds(pl.multiple_of((1 - depth) * hidden, 128), hidden)] = b_x[...]
    bgrad_ref[...] = b_all[...].reshape(2 * hidden)
    for copy in kept:
        copy.wait()
    for copy in sends:
        copy.wait_send()


def weight_kernel(
    tok_ref, og_ref, act_ref, hg_ref, out_ref, bgrad_ref,
    w_in_grad_ref, w_out_grad_ref, out_again, bgrad_again, tok_turned,
):
    @pl.when(pl.program_id(0) == 0)
    def _():
        tok_turned[...] = tok_ref[...].T
        out_again[...] = out_ref[...]
        bgrad_again[...] = bgrad_ref[...]

    w_in_grad_ref[...] = jnp.dot(tok_turned[...], hg_ref[...], preferred_element_type=F32).astype(BF16)
    w_out_grad_ref[...] = left_transposed(act_ref[...], og_ref[...]).astype(BF16)


def fused(col_count, tokens, out_grad, w_in, b_in, w_out):
    tile_rows, feats = tokens.shape
    hidden = w_in.shape[1] // 2
    plane = col_count * tile_rows
    half = tile_rows // 2
    rows = 2 * plane
    anywhere = pl.BlockSpec(memory_space=pltpu.HBM)
    vmem = pl.BlockSpec(memory_space=pltpu.VMEM)
    dma = pltpu.SemaphoreType.DMA
    outs = pl.pallas_call(
        functools.partial(block_kernel, col_count),
        out_shape=[
            jax.ShapeDtypeStruct((tile_rows, feats), BF16),
            jax.ShapeDtypeStruct((tile_rows, feats), F32),
            jax.ShapeDtypeStruct((2 * hidden,), F32),
            jax.ShapeDtypeStruct((2, col_count, tile_rows, feats), BF16),
            jax.ShapeDtypeStruct((2, col_count, tile_rows, feats), BF16),
            jax.ShapeDtypeStruct((2, col_count, 2, half, hidden), BF16),
            jax.ShapeDtypeStruct((2, col_count, 2, half, hidden), BF16),
        ] + [jax.ShapeDtypeStruct((tile_rows, feats), BF16)] * (col_count - 1),
        in_specs=[anywhere] * 5,
        out_specs=[vmem, vmem, vmem, anywhere, anywhere, anywhere, anywhere] + [vmem] * (col_count - 1),
        scratch_shapes=[
            pltpu.VMEM((2, col_count, tile_rows, feats), BF16),
            pltpu.VMEM((2, col_count, tile_rows, feats), BF16),
            pltpu.VMEM((feats, hidden), BF16),
            pltpu.VMEM((hidden, feats), BF16),
            pltpu.VMEM((2 * hidden,), F32),
            pltpu.VMEM((1, 2 * hidden), F32),
            pltpu.VMEM((2, 2, 2, col_count, half, hidden), F32),
            pltpu.VMEM((2, 2, 2, col_count, half, hidden), BF16),
            pltpu.VMEM((2, 2, col_count, half, hidden), BF16),
            pltpu.VMEM((2, 2, col_count, half, hidden), BF16),
            pltpu.VMEM((2, 2, col_count, half, hidden), BF16),
            pltpu.VMEM((2, col_count, 2, half, hidden), BF16),
            pltpu.VMEM((2, col_count, 2, half, hidden), BF16),
            pltpu.VMEM((2, col_count, half, hidden), F32),
            pltpu.VMEM((2, col_count, tile_rows, feats), BF16),
            pltpu.VMEM((2, col_count, tile_rows, feats), BF16),
            pltpu.VMEM((2, col_count, tile_rows, feats), F32),
            pltpu.VMEM((2, col_count, tile_rows, feats), BF16),
            pltpu.VMEM((2, col_count - 1, tile_rows, feats), BF16),
            pltpu.VMEM((1, hidden), F32),
            pltpu.VMEM((1, hidden), F32),
            pltpu.VMEM((1, hidden), F32),
            pltpu.VMEM((1, hidden), F32),
            dma((5,)),
            dma((2, col_count)),
            dma((2, col_count)),
            dma((2, col_count)),
            dma((2, col_count)),
            dma((2, 3)),
            dma((2, 3)),
            dma((2, 3)),
            dma((2, 3)),
            dma((2, 3)),
            dma((2, 3)),
            dma((2,)),
            dma((2,)),
            dma((2, col_count - 1)),
            dma((2, col_count - 1)),
            dma((2,)),
            dma((2,)),
            dma((4,)),
        ],
        compiler_params=pltpu.CompilerParams(
            collective_id=0, has_side_effects=True, vmem_limit_bytes=44 * 2**20
        ),
        cost_estimate=pl.CostEstimate(
            flops=8 * rows * feats * hidden, bytes_accessed=8 * feats * hidden, transcendentals=rows * hidden
        ),
    )(tokens, out_grad, w_in, b_in, w_out)
    block_out, tokens_part, bias_grad, tok, og, act, hg = outs[:7]
    arrived = []
    for step, piece in enumerate(outs[7:], 1):
        to_peer = [(c, (c + step) % col_count) for c in range(col_count)]
        arrived.append(lax.ppermute(piece, "col", to_peer))
    whole_block = lambda i: (0, 0)
    w_in_grad, w_out_grad, block_out, bias_grad = pl.pallas_call(
        weight_kernel,
        grid=(hidden // TILE,),
        out_shape=[
            jax.ShapeDtypeStruct((feats, hidden), BF16),
            jax.ShapeDtypeStruct((hidden, feats), BF16),
            jax.ShapeDtypeStruct((tile_rows, feats), BF16),
            jax.ShapeDtypeStruct((2 * hidden,), F32),
        ],
        in_specs=[
            pl.BlockSpec((rows, feats), whole_block),
            pl.BlockSpec((rows, feats), whole_block),
            pl.BlockSpec((rows, TILE), lambda i: (0, i)),
            pl.BlockSpec((rows, TILE), lambda i: (0, i)),
            pl.BlockSpec((tile_rows, feats), whole_block),
            pl.BlockSpec((2 * hidden,), lambda i: (0,)),
        ],
        out_specs=[
            pl.BlockSpec((feats, TILE), lambda i: (0, i)),
            pl.BlockSpec((TILE, feats), lambda i: (i, 0)),
            pl.BlockSpec((tile_rows, feats), whole_block),
            pl.BlockSpec((2 * hidden,), lambda i: (0,)),
        ],
        scratch_shapes=[pltpu.VMEM((feats, rows), BF16)],
        compiler_params=pltpu.CompilerParams(vmem_limit_bytes=44 * 2**20),
        cost_estimate=pl.CostEstimate(
            flops=4 * rows * feats * hidden, bytes_accessed=4 * feats * hidden, transcendentals=0
        ),
    )(
        tok.reshape(rows, feats), og.reshape(rows, feats), act.reshape(rows, hidden), hg.reshape(rows, hidden),
        block_out, bias_grad,
    )
    tokens_grad = tokens_part
    for piece in arrived:
        tokens_grad = tokens_grad + piece.astype(F32)
    tokens_grad = tokens_grad.astype(BF16)
    return block_out, tokens_grad, w_in_grad, w_out_grad, bias_grad


def by_shape(mesh):
    def run(tokens, out_grad, w_in, b_in, w_out):
        depth_count = mesh.shape["depth"]
        fits = (
            mesh.shape["row"] == 4
            and depth_count == 2
            and mesh.shape["col"] > 1
            and tokens.shape[0] % 32 == 0
            and tokens.shape[1] % TILE == 0
            and w_in.shape[1] % (depth_count * TILE) == 0
        )
        if fits:
            return fused(mesh.shape["col"], tokens, out_grad, w_in, b_in, w_out)
        return local(tokens, out_grad, w_in, b_in, w_out)

    return run


def solution(mesh):
    return jax.shard_map(
        by_shape(mesh),
        mesh=mesh,
        in_specs=(
            P(("col", "depth"), "row"),
            P(("col", "depth"), "row"),
            P("row", "col"),
            P("col"),
            P("col", "row"),
        ),
        out_specs=(
            P(("col", "depth"), "row"),
            P(("col", "depth"), "row"),
            P("row", ("col", "depth")),
            P(("col", "depth"), "row"),
            P("col"),
        ),
        check_vma=False,
    )
```
